768 devices in a mesh: row: 24 (over z, x_hi), col: 32 (over y, x_lo, core).
Axes of the slice: x: 4 (x_hi: 2, x_lo: 2; x = x_hi * 2 + x_lo), y: 8, z: 12, core: 2. Of those that a mesh axis runs over, the one named last changes fastest.
Arguments:
- a_vals: bfloat16 [24, 32, 32, 256, 256], P('row', 'col'), may hold values from -1 to 1
- a_place: int32 [24, 32, 2, 32], P('row', 'col'), may hold values from 0 to 31, as said below
- a_count: int32 [24, 32], P('row', 'col'), may hold values from 8 to 32, as said below
- p_cols: int32 [768, 2], replicated, may hold values from 0 to 7, all different within a row
- r_cols: int32 [768, 2], replicated, may hold values from 0 to 7, all different within a row
- null_layout: int32 [64], replicated, may hold values from 0 to 63, each once
- mass: float32 [768, 256], P(('row', 'col')), may hold values from 1 to 2
- p_now: bfloat16 [768, 256, 128], P(('row', 'col')), may hold values from -4 to 4
- res_p: bfloat16 [768, 256, 128], P(('row', 'col')), may hold values from -60 to 60
- rt_now: bfloat16 [768, 256, 128], P(('row', 'col')), may hold values from -4 to 4
- res_r: bfloat16 [768, 256, 128], P(('row', 'col')), may hold values from -60 to 60
Outputs:
- p_next: bfloat16 [768, 256, 128], P(('row', 'col'))
- res_p_next: bfloat16 [768, 256, 128], P(('row', 'col'))
- rt_next: bfloat16 [768, 256, 128], P(('row', 'col'))
- res_r_next: bfloat16 [768, 256, 128], P(('row', 'col'))
The draws below stay inside these ranges and needn't reach their ends.
Inputs may be any that keep to these rules, and one draw needn't show every extreme that they name: Slots 0 to a_count[r, c] - 1 of device block (r, c) are live; some device block has exactly 32. `a_place`: entry 0 is below 32, entry 1 below 24; the slots of one device block hold distinct positions.
All inputs are finite; a program needn't handle non-finite values.
Results may differ from the reference program's by a relative error of at most 0.015.
Values may be sent and summed in bfloat16 or wider, within the bound.
No kernel may reach another device: no remote copies, remote signals or barrier semaphores. Data moves between devices by JAX's collectives and lax.ppermute only.
A program may use at most 64 MiB of HBM per device.

```python
import math
import jax
import jax.numpy as jnp
from jax import lax

TILE = 256
CW = 64
KP = 2
NS = 4
NCT = 8
SLOTS = 32
NT = 768
N_ROW = 24
N_COL = 32


def draw_a_count(key, part):
    key = jax.random.fold_in(key, 11)
    first_key, second_key, third_key = jax.random.split(key, 3)
    blocks_all = N_ROW * N_COL
    full_block = jax.random.randint(first_key, (blocks_all,), 0, 8) == 0
    light_load = jax.random.randint(second_key, (blocks_all,), SLOTS // 4, SLOTS // 2 + 1)
    counts = jnp.where(full_block, SLOTS, light_load)
    forced = jax.random.randint(third_key, (), 0, blocks_all)
    counts = jnp.where(jnp.arange(blocks_all) == forced, SLOTS, counts)
    return counts.reshape(N_ROW, N_COL).astype(jnp.int32)


def draw_a_place(key, part):
    key = jax.random.fold_in(key, 12)
    positions = N_ROW * N_COL
    block_keys = jax.random.split(key, positions)

    def one_block(block_key):
        ordering = jax.random.permutation(block_key, positions)[:SLOTS]
        return jnp.stack([ordering // N_ROW, ordering % N_ROW])
    places = jax.vmap(one_block)(block_keys)
    return places.reshape(N_ROW, N_COL, 2, SLOTS).astype(jnp.int32)


def draw_a_vals(key, part):
    key = jax.random.fold_in(key, 13)
    blocks_all = N_ROW * N_COL
    spread = (SLOTS * TILE // 2) ** (-0.5)

    def one_block(index):
        block_key = jax.random.fold_in(key, index)
        noise_key, level_key = jax.random.split(block_key)
        noise = jnp.clip(jax.random.normal(noise_key, (SLOTS, TILE, TILE)), -4.0, 4.0) * spread
        level = jnp.exp(jax.random.uniform(level_key, (SLOTS, 1, 1), minval=math.log(1.5), maxval=math.log(4.0))) / TILE
        return (noise + level).astype(jnp.bfloat16)
    values = lax.map(one_block, jnp.arange(blocks_all, dtype=jnp.int32))
    return values.reshape(N_ROW, N_COL, SLOTS, TILE, TILE)


def shaped_field(key, base, spread):
    first_key, second_key = jax.random.split(key)
    tile_total = base.shape[0]
    position = jnp.arange(tile_total).astype(jnp.float32) / max(tile_total - 1, 1)
    trend = (3.0 ** (spread * position))[:, None, None]
    row_scale = jnp.exp(jax.random.uniform(first_key, (tile_total, base.shape[1], 1), minval=math.log(0.3), maxval=math.log(3.0)))
    col_scale = jnp.exp(jax.random.uniform(second_key, (1, 1, base.shape[2]), minval=math.log(0.3), maxval=math.log(3.0)))
    return jnp.clip(base * trend * row_scale * col_scale, -60.0, 60.0)


def residual_draw(key, strength):
    first_key, second_key, third_key = jax.random.split(key, 3)
    shape = (N_ROW * N_COL, TILE, KP * CW)
    offset = jnp.tile(jnp.clip(jax.random.normal(second_key, (CW,)), -3.0, 3.0), KP)[None, None, :]
    base = jnp.clip(jax.random.normal(first_key, shape), -4.0, 4.0) + strength * offset
    return shaped_field(third_key, base, 0.5).astype(jnp.bfloat16)


def draw_res_p(key, part):
    key = jax.random.fold_in(key, 21)
    return residual_draw(key, 1.0)


def draw_res_r(key, part):
    key = jax.random.fold_in(key, 22)
    return residual_draw(key, 0.2)


def levels(rng, extent, cuts, low, high):
    factor_of = 1.0
    for dim, shards_of in cuts:
        steps = jax.random.uniform(jax.random.fold_in(jax.random.fold_in(rng, 6), dim), (shards_of,), jnp.float32, low / len(cuts), high / len(cuts))
        factor_of = factor_of * jnp.repeat(jnp.exp(steps), extent[dim] // shards_of).reshape((-1,) + (1,) * (len(extent) - 1 - dim))
    return factor_of


def distinct(rng, rows, number_of, top, lift):
    order = jax.random.permutation(jax.random.fold_in(rng, 1), number_of)
    pull = order
    for power in range(3):
        pull = pull * pull // number_of
    pull = pull * lift // number_of
    lots = jax.random.randint(jax.random.fold_in(rng, 2), (rows, number_of), 0, 4096) + pull
    fixed_rows = jax.random.permutation(jax.random.fold_in(rng, 3), rows)[jnp.arange(number_of) % rows]
    lots = jnp.where(jnp.arange(rows)[:, None] == fixed_rows[None, :], 1 << 14, lots)
    merit = lots * number_of + jnp.arange(number_of)
    return lax.top_k(merit.astype(jnp.int32), top)[1].astype(jnp.int32)


def normal_values(key, shape, scale, reach, pieces=(), kind=jnp.bfloat16):
    drawn = jax.random.normal(key, shape, jnp.float32) * scale
    if len(pieces) > 0:
        drawn = levels(key, shape, pieces, -0.22, 0.18) * drawn
    return jnp.clip(drawn, min=-reach, max=reach).astype(kind)


def setup_inputs(seed: int = 0) -> dict:
    arg_keys = jax.random.split(jax.random.key(seed), 12)
    a_vals = draw_a_vals(jax.random.fold_in(arg_keys[11], 71), 0)
    a_place = draw_a_place(jax.random.fold_in(arg_keys[11], 71), 0)
    a_count = draw_a_count(jax.random.fold_in(arg_keys[11], 71), 0)
    p_cols = distinct(arg_keys[3], NT, NCT, KP, 0)
    r_cols = distinct(arg_keys[4], NT, NCT, KP, 0)
    null_layout = jax.random.permutation(arg_keys[5], CW).astype(jnp.int32)
    mass = jnp.clip(jnp.exp(math.log(2.0) - 0.6931472 * jax.random.uniform(arg_keys[6], (NT, TILE), jnp.float32) ** levels(arg_keys[6], (NT, TILE), ((0, 768),), -0.2, 0.2)), 1.0, 2.0)
    p_now = normal_values(arg_keys[7], (NT, TILE, KP * CW), 1.0, 4.0, ((0, 768),))
    res_p = draw_res_p(jax.random.fold_in(arg_keys[11], 71), 0)
    rt_now = normal_values(arg_keys[9], (NT, TILE, KP * CW), 1.0, 4.0, ((0, 768),))
    res_r = draw_res_r(jax.random.fold_in(arg_keys[11], 71), 0)
    return dict(a_vals=a_vals, a_place=a_place, a_count=a_count, p_cols=p_cols, r_cols=r_cols, null_layout=null_layout, mass=mass, p_now=p_now, res_p=res_p, rt_now=rt_now, res_r=res_r)


EXACT_DOTS = lax.Precision.HIGHEST
EPSILON = 1e-6


def projector(null_layout):
    component = jnp.tile(null_layout % NS, KP)
    same_group = (component[:, None] == component[None, :]).astype(jnp.float32)
    return same_group * (NS / (KP * CW))


def pick_blocks(tile_set, source, target, live_slot):
    matched = ((source[:, :, None] == target[:, None, :]) & live_slot[:, None, None]).astype(jnp.float32)
    split_tiles = tile_set.astype(jnp.float32).reshape(SLOTS, TILE, KP, CW)
    picked = jnp.einsum('ats,axty->axsy', matched, split_tiles, precision=EXACT_DOTS)
    return picked.reshape(SLOTS, TILE, KP * CW).astype(jnp.bfloat16)


def block_terms(number, flat_vals, flat_place, flat_count, p_cols, r_cols, res_p, res_r):
    row_id = number // N_COL
    col_id = number % N_COL
    tile_vals = lax.dynamic_index_in_dim(flat_vals, number, 0, keepdims=False).astype(jnp.float32)
    place_now = lax.dynamic_index_in_dim(flat_place, number, 0, keepdims=False)
    count_now = lax.dynamic_index_in_dim(flat_count, number, 0, keepdims=False)
    local_row = place_now[0]
    local_col = place_now[1]
    live_slot = jnp.arange(SLOTS, dtype=jnp.int32) < count_now
    tile_row = row_id * N_COL + local_row
    tile_col = local_col * N_COL + col_id
    prolong_pick = pick_blocks(res_p[tile_col], p_cols[tile_col], p_cols[tile_row], live_slot)
    prolong_prod = jnp.einsum('axy,ayz->axz', tile_vals, prolong_pick.astype(jnp.float32), precision=EXACT_DOTS)
    row_select = (local_row[None, :] == jnp.arange(N_COL, dtype=jnp.int32)[:, None]).astype(jnp.float32)
    prolong_part = jnp.einsum('la,axz->lxz', row_select, prolong_prod, precision=EXACT_DOTS).astype(jnp.bfloat16)
    restrict_pick = pick_blocks(res_r[tile_row], r_cols[tile_row], r_cols[tile_col], live_slot)
    restrict_prod = jnp.einsum('axy,axz->ayz', tile_vals, restrict_pick.astype(jnp.float32), precision=EXACT_DOTS)
    col_select = (local_col[None, :] == jnp.arange(N_ROW, dtype=jnp.int32)[:, None]).astype(jnp.float32)
    restrict_part = jnp.einsum('la,ayz->lyz', col_select, restrict_prod, precision=EXACT_DOTS).astype(jnp.bfloat16)
    return prolong_part, restrict_part


def reference(a_vals, a_place, a_count, p_cols, r_cols, null_layout, mass, p_now, res_p, rt_now, res_r):
    tile_total = N_ROW * N_COL
    block_width = KP * CW
    flat_vals = a_vals.reshape(tile_total, SLOTS, TILE, TILE)
    flat_place = a_place.reshape(tile_total, 2, SLOTS)
    flat_count = a_count.reshape(tile_total)

    def visit(number, running):
        number = jnp.asarray(number).astype(jnp.int32)
        prolong_sum, restrict_sum = running
        prolong_part, restrict_part = block_terms(number, flat_vals, flat_place, flat_count, p_cols, r_cols, res_p, res_r)
        row_id = number // N_COL
        col_id = number % N_COL
        prolong_row = lax.dynamic_index_in_dim(prolong_sum, row_id, 0, keepdims=False) + prolong_part.astype(jnp.float32)
        prolong_sum = lax.dynamic_update_index_in_dim(prolong_sum, prolong_row, row_id, 0)
        restrict_col = lax.dynamic_index_in_dim(restrict_sum, col_id, 1, keepdims=False) + restrict_part.astype(jnp.float32)
        restrict_sum = lax.dynamic_update_index_in_dim(restrict_sum, restrict_col, col_id, 1)
        return prolong_sum, restrict_sum

    empty_sum = jnp.zeros((N_ROW, N_COL, TILE, block_width), jnp.float32)
    prolong_sum, restrict_sum = lax.fori_loop(0, tile_total, visit, (empty_sum, empty_sum))
    projector_m = projector(null_layout)
    mass_rows = mass.astype(jnp.float32)[:, :, None]
    resid_p = res_p.astype(jnp.float32)
    resid_r = res_r.astype(jnp.float32)
    prolong_full = prolong_sum.reshape(tile_total, TILE, block_width) + mass_rows * resid_p
    restrict_full = restrict_sum.reshape(tile_total, TILE, block_width) + mass_rows * resid_r
    update_p = prolong_full - jnp.einsum('txy,yz->txz', prolong_full, projector_m, precision=EXACT_DOTS)
    update_r = restrict_full - jnp.einsum('txy,yz->txz', restrict_full, projector_m, precision=EXACT_DOTS)
    alpha_p = jnp.sum(update_p * resid_p) / (jnp.sum(update_p * update_p) + EPSILON)
    alpha_r = jnp.sum(update_r * resid_r) / (jnp.sum(update_r * update_r) + EPSILON)
    p_next = (p_now.astype(jnp.float32) + alpha_p * resid_p).astype(jnp.bfloat16)
    res_p_next = (resid_p - alpha_p * update_p).astype(jnp.bfloat16)
    rt_next = (rt_now.astype(jnp.float32) + alpha_r * resid_r).astype(jnp.bfloat16)
    res_r_next = (resid_r - alpha_r * update_r).astype(jnp.bfloat16)
    return p_next, res_p_next, rt_next, res_r_next
```

```python
import functools

import jax
import jax.numpy as jnp
from jax import lax
from jax.experimental import pallas as pl
from jax.experimental.pallas import tpu as pltpu
from jax.sharding import Mesh
from jax.sharding import PartitionSpec as P

NS = 4
EPSILON = 1e-06
EXACT = lax.Precision.HIGHEST

SIZES = (12, 2, 8, 2, 2)
AXES = ("z", "xh", "y", "xl", "core")
N_Z, N_XH, N_Y, N_XL, N_CORE = SIZES
N_ROW, N_COL = N_Z * N_XH, N_Y * N_XL * N_CORE
HALF_COL = N_COL // 2
SWAP = ((0, 1), (1, 0))

VMEM = pl.BlockSpec(memory_space=pltpu.VMEM)
SMEM = pl.BlockSpec(memory_space=pltpu.SMEM)
PARAMS = pltpu.CompilerParams(vmem_limit_bytes=48 * 1024 * 1024)


def pick_columns(tile, straight, crossed):
    block = tile.shape[1] // 2
    lane = lax.broadcasted_iota(jnp.int32, tile.shape, 1)
    left = lane < block
    wide = tile.astype(jnp.float32)
    turned = pltpu.roll(wide, block, 1)
    as_is = jnp.where(left, straight[0], straight[1]) != 0
    other = jnp.where(left, crossed[0], crossed[1]) != 0
    picked = jnp.where(as_is, wide, jnp.where(other, turned, 0.0))
    return picked.astype(jnp.bfloat16)


def matches(cols_ref, source, target):
    s0, s1 = cols_ref[2 * source], cols_ref[2 * source + 1]
    t0, t1 = cols_ref[2 * target], cols_ref[2 * target + 1]
    flag = lambda same: same.astype(jnp.int32)
    return (flag(s0 == t0), flag(s1 == t1)), (flag(s1 == t0), flag(s0 == t1))


def clear(acc_ref):
    def body(i, carry):
        acc_ref[i] = jnp.zeros(acc_ref.shape[1:], acc_ref.dtype)
        return carry

    lax.fori_loop(0, acc_ref.shape[0], body, 0)


def prolong_kernel(where_ref, place_ref, cols_ref, a_ref, tiles_ref, mine_ref, theirs_ref, acc_ref):
    count, xh, core = where_ref[0], where_ref[1], where_ref[2]
    row_id, col_id = where_ref[3], where_ref[4]
    slots = a_ref.shape[0]
    clear(acc_ref)

    def body(a, carry):
        local_row, local_col = place_ref[a], place_ref[slots + a]
        straight, crossed = matches(
            cols_ref, local_col * N_COL + col_id, row_id * N_COL + local_row
        )

        @pl.when(straight[0] + straight[1] + crossed[0] + crossed[1] > 0)
        def _():
            tile = tiles_ref[local_col // 2, jnp.where(local_col % 2 == xh, 0, 1)]
            picked = pick_columns(tile, straight, crossed)
            acc_ref[local_row] += jnp.dot(a_ref[a], picked, preferred_element_type=jnp.float32)

        return carry

    lax.fori_loop(0, count, body, 0)

    def store(q, carry):
        mine_ref[q] = acc_ref[2 * q + core].astype(jnp.bfloat16)
        theirs_ref[q] = acc_ref[2 * q + 1 - core].astype(jnp.bfloat16)
        return carry

    lax.fori_loop(0, HALF_COL, store, 0)


def restrict_kernel(
    where_ref, place_ref, cols_ref, a_ref, own_ref, other_ref, mine_ref, theirs_ref, acc_ref
):
    count, xh, core = where_ref[0], where_ref[1], where_ref[2]
    row_id, col_id, xl = where_ref[3], where_ref[4], where_ref[5]
    slots = a_ref.shape[0]
    clear(acc_ref)

    def body(a, carry):
        local_row, local_col = place_ref[a], place_ref[slots + a]
        straight, crossed = matches(
            cols_ref, row_id * N_COL + local_row, local_col * N_COL + col_id
        )

        @pl.when(straight[0] + straight[1] + crossed[0] + crossed[1] > 0)
        def _():
            y, chip = local_row // 4, jnp.where((local_row // 2) % 2 == xl, 0, 1)

            def add(tile):
                picked = pick_columns(tile, straight, crossed)
                acc_ref[local_col] += lax.dot_general(
                    a_ref[a],
                    picked,
                    (((0,), (0,)), ((), ())),
                    preferred_element_type=jnp.float32,
                )

            @pl.when(local_row % 2 == core)
            def _():
                add(own_ref[y, chip])

            @pl.when(local_row % 2 != core)
            def _():
                add(other_ref[y, chip])

        return carry

    lax.fori_loop(0, count, body, 0)

    def store(z, carry):
        mine_ref[z] = acc_ref[2 * z + xh].astype(jnp.bfloat16)
        theirs_ref[z] = acc_ref[2 * z + 1 - xh].astype(jnp.bfloat16)
        return carry

    lax.fori_loop(0, N_Z, store, 0)


def update_kernel(parts_ref, mass_ref, resid_ref, projector_ref, update_ref, sums_ref):
    def body(i, total):
        return total + parts_ref[i].astype(jnp.float32)

    resid = resid_ref[...].astype(jnp.float32)
    full = mass_ref[...] * resid
    full = lax.fori_loop(0, parts_ref.shape[0], body, full)
    update = full - jnp.dot(
        full, projector_ref[...], precision=EXACT, preferred_element_type=jnp.float32
    )
    update_ref[...] = update
    sums_ref[0:1, :] = jnp.sum(update * resid, axis=0, keepdims=True)
    sums_ref[1:2, :] = jnp.sum(update * update, axis=0, keepdims=True)


def shape(dims, dtype=jnp.bfloat16):
    return jax.ShapeDtypeStruct(dims, dtype)


def step(parts, mass_rows, resid, projector):
    return pl.pallas_call(
        update_kernel,
        out_shape=(shape(resid.shape, jnp.float32), shape((2, resid.shape[1]), jnp.float32)),
        in_specs=[VMEM] * 4,
        out_specs=(VMEM, VMEM),
        compiler_params=PARAMS,
    )(parts, mass_rows, resid, projector)


def sum_over(values, axes, count):
    spread = jnp.broadcast_to(values[None], (count,) + values.shape)
    return jnp.sum(lax.all_to_all(spread, axes, 0, 0, tiled=True), axis=0)


def shards(
    a_vals, a_place, a_count, p_cols, r_cols, null_layout, mass, p_now, res_p, rt_now, res_r
):
    z, xh, y, xl, core = (lax.axis_index(name) for name in AXES)
    row_id = z * N_XH + xh
    col_id = (y * N_XL + xl) * N_CORE + core
    where = jnp.stack([a_count[0, 0], xh, core, row_id, col_id, xl]).astype(jnp.int32)
    tile_vals = a_vals[0, 0]
    place = a_place[0, 0].reshape(-1)
    slots, height = tile_vals.shape[:2]
    width = res_p.shape[2]
    p_flat, r_flat = p_cols.reshape(-1), r_cols.reshape(-1)

    near = lax.ppermute(res_p, "xh", SWAP)
    p_rows = lax.all_gather(jnp.stack([res_p[0], near[0]]), "z", axis=0)
    near = lax.ppermute(res_r, "xl", SWAP)
    pair = jnp.stack([res_r[0], near[0]])
    r_own = lax.all_to_all(
        jnp.broadcast_to(pair[None], (N_Y,) + pair.shape), "y", 0, 0, tiled=True
    )
    r_other = lax.ppermute(r_own, "core", SWAP)

    r_mine, r_theirs = pl.pallas_call(
        restrict_kernel,
        out_shape=(shape((N_Z, height, width)),) * 2,
        in_specs=[SMEM] * 3 + [VMEM] * 3,
        out_specs=(VMEM, VMEM),
        scratch_shapes=[pltpu.VMEM((N_ROW, height, width), jnp.float32)],
        compiler_params=PARAMS,
    )(where, place, r_flat, tile_vals, r_own, r_other)
    r_near = lax.ppermute(r_theirs, "xh", SWAP)
    r_sum = (r_mine.astype(jnp.float32) + r_near.astype(jnp.float32)).astype(jnp.bfloat16)
    r_part = lax.psum_scatter(r_sum, "z", scatter_dimension=0, tiled=True)

    p_mine, p_theirs = pl.pallas_call(
        prolong_kernel,
        out_shape=(shape((HALF_COL, height, width)),) * 2,
        in_specs=[SMEM] * 3 + [VMEM] * 2,
        out_specs=(VMEM, VMEM),
        scratch_shapes=[pltpu.VMEM((N_COL, height, width), jnp.float32)],
        compiler_params=PARAMS,
    )(where, place, p_flat, tile_vals, p_rows)
    p_near = lax.ppermute(p_theirs, "core", SWAP)
    p_sum = (p_mine.astype(jnp.float32) + p_near.astype(jnp.float32)).astype(jnp.bfloat16)
    p_part = lax.all_to_all(p_sum, ("y", "xl"), 0, 0, tiled=True)

    component = jnp.tile(null_layout % NS, width // null_layout.shape[0])
    projector = (component[:, None] == component[None, :]).astype(jnp.float32) * (NS / width)
    mass_rows = mass[0][:, None]
    update_p, sums_p = step(p_part, mass_rows, res_p[0], projector)
    update_r, sums_r = step(r_part, mass_rows, res_r[0], projector)
    sums = jnp.sum(jnp.concatenate([sums_p, sums_r]), axis=1)
    sums = jnp.pad(sums[None], ((0, 0), (0, width - sums.shape[0])))
    sums = sum_over(sums, ("y", "xl", "core"), N_COL)
    sums = sum_over(sums, ("z", "xh"), N_ROW)[0]
    alpha_p = sums[0] / (sums[1] + EPSILON)
    alpha_r = sums[2] / (sums[3] + EPSILON)
    resid_p, resid_r = res_p[0].astype(jnp.float32), res_r[0].astype(jnp.float32)
    p_next = (p_now[0].astype(jnp.float32) + alpha_p * resid_p).astype(jnp.bfloat16)
    res_p_next = (resid_p - alpha_p * update_p).astype(jnp.bfloat16)
    rt_next = (rt_now[0].astype(jnp.float32) + alpha_r * resid_r).astype(jnp.bfloat16)
    res_r_next = (resid_r - alpha_r * update_r).astype(jnp.bfloat16)
    return (p_next[None], res_p_next[None], rt_next[None], res_r_next[None])


def solution(mesh):
    fine = Mesh(mesh.devices.reshape(SIZES), AXES)
    row, col = ("z", "xh"), ("y", "xl", "core")
    tiles = P(row + col, None, None)
    in_specs = (
        P(row, col, None, None, None),
        P(row, col, None, None),
        P(row, col),
        P(),
        P(),
        P(),
        P(row + col, None),
        tiles,
        tiles,
        tiles,
        tiles,
    )
    return jax.shard_map(
        shards, mesh=fine, in_specs=in_specs, out_specs=(tiles,) * 4, check_vma=False
    )
```

```python
import functools

import jax
import jax.numpy as jnp
from jax import lax
from jax.experimental import pallas as pl
from jax.experimental.pallas import tpu as pltpu
from jax.sharding import Mesh
from jax.sharding import PartitionSpec as P

NS = 4
EPSILON = 1e-06
EXACT = lax.Precision.HIGHEST

SIZES = (12, 2, 8, 2, 2)
AXES = ("z", "xh", "y", "xl", "core")
N_Z, N_XH, N_Y, N_XL, N_CORE = SIZES
N_ROW, N_COL = N_Z * N_XH, N_Y * N_XL * N_CORE
HALF_COL = N_COL // 2
SWAP = ((0, 1), (1, 0))

VMEM = pl.BlockSpec(memory_space=pltpu.VMEM)
SMEM = pl.BlockSpec(memory_space=pltpu.SMEM)
COST = pl.CostEstimate(flops=2**29, bytes_accessed=12 * 2**20, transcendentals=0)
MIB = 2**20


def pick_columns(tile, straight, crossed):
    block = tile.shape[1] // 2
    lane = lax.broadcasted_iota(jnp.int32, tile.shape, 1)
    left = lane < block
    wide = tile.astype(jnp.float32)
    turned = pltpu.roll(wide, block, 1)
    as_is = jnp.where(left, straight[0], straight[1]) != 0
    other = jnp.where(left, crossed[0], crossed[1]) != 0
    picked = jnp.where(as_is, wide, jnp.where(other, turned, 0.0))
    return picked.astype(jnp.bfloat16)


def matches(cols_ref, source, target):
    s0, s1 = cols_ref[2 * source], cols_ref[2 * source + 1]
    t0, t1 = cols_ref[2 * target], cols_ref[2 * target + 1]
    flag = lambda same: same.astype(jnp.int32)
    return (flag(s0 == t0), flag(s1 == t1)), (flag(s1 == t0), flag(s0 == t1))


def clear(acc_ref):
    def body(i, carry):
        acc_ref[i] = jnp.zeros(acc_ref.shape[1:], acc_ref.dtype)
        return carry

    lax.fori_loop(0, acc_ref.shape[0], body, 0)


def each_match(where_ref, place_ref, cols_ref, slots, turn, product):
    count, row_id, col_id = where_ref[0], where_ref[3], where_ref[4]

    def body(a, carry):
        local_row, local_col = place_ref[a], place_ref[slots + a]
        tile_row = row_id * N_COL + local_row
        tile_col = local_col * N_COL + col_id
        source, target = (tile_row, tile_col) if turn else (tile_col, tile_row)
        straight, crossed = matches(cols_ref, source, target)

        @pl.when(straight[0] + straight[1] + crossed[0] + crossed[1] > 0)
        def _():
            product(a, local_row, local_col, straight, crossed)

        return carry

    lax.fori_loop(0, count, body, 0)


def fetch(tile_ref, choices):
    for holds, ref, index in choices:

        @pl.when(holds)
        def _(ref=ref, index=index):
            tile_ref[...] = ref[index]


def prolong_kernel(
    where_ref,
    place_ref,
    cols_ref,
    a_ref,
    own_ref,
    up_ref,
    down_ref,
    near_own_ref,
    near_up_ref,
    near_down_ref,
    mine_ref,
    theirs_low_ref,
    theirs_high_ref,
    acc_ref,
    tile_ref,
):
    xh, core, z = where_ref[1], where_ref[2], where_ref[5]
    clear(acc_ref)

    def product(a, local_row, local_col, straight, crossed):
        here = lax.rem(local_col, N_XH) == xh
        ahead = lax.rem(local_col // N_XH - z + N_Z, N_Z)
        third = lax.rem(ahead, 3)
        choices = []
        for side, refs in (
            (here, (own_ref, up_ref, down_ref)),
            (jnp.logical_not(here), (near_own_ref, near_up_ref, near_down_ref)),
        ):
            for k, offset in enumerate((0, 1, -1)):
                index = lax.rem(ahead - offset + N_Z, N_Z) // 3
                choices.append((side & (third == k), refs[k], index))
        fetch(tile_ref, choices)
        picked = pick_columns(tile_ref[...], straight, crossed)
        acc_ref[local_row] += jnp.dot(a_ref[a], picked, preferred_element_type=jnp.float32)

    each_match(where_ref, place_ref, cols_ref, a_ref.shape[0], False, product)

    def store(q, carry):
        mine_ref[q] = acc_ref[2 * q + core].astype(jnp.bfloat16)
        return carry

    lax.fori_loop(0, HALF_COL, store, 0)

    def store_theirs(q, carry):
        theirs_low_ref[q] = acc_ref[2 * q + 1 - core].astype(jnp.bfloat16)
        theirs_high_ref[q] = acc_ref[HALF_COL + 2 * q + 1 - core].astype(jnp.bfloat16)
        return carry

    lax.fori_loop(0, HALF_COL // 2, store_theirs, 0)


def restrict_kernel(
    where_ref,
    place_ref,
    cols_ref,
    a_ref,
    own_ref,
    other_ref,
    mine_ref,
    theirs_ref,
    after_ref,
    acc_ref,
    tile_ref,
):
    for i in range(where_ref.shape[0]):
        after_ref[i] = where_ref[i]
    xh, core, z = where_ref[1], where_ref[2], where_ref[5]
    clear(acc_ref)

    def product(a, local_row, local_col, straight, crossed):
        here = lax.rem(local_row, N_CORE) == core
        index = local_row // N_CORE
        fetch(tile_ref, [(here, own_ref, index), (jnp.logical_not(here), other_ref, index)])
        picked = pick_columns(tile_ref[...], straight, crossed)
        acc_ref[local_col] += lax.dot_general(
            a_ref[a], picked, (((0,), (0,)), ((), ())), preferred_element_type=jnp.float32
        )

    each_match(where_ref, place_ref, cols_ref, a_ref.shape[0], True, product)

    def store(q, carry):
        owner = 3 * lax.rem(q, 4) + lax.rem(z + q // 4, 3)
        mine_ref[q] = acc_ref[2 * owner + xh].astype(jnp.bfloat16)
        theirs_ref[q] = acc_ref[2 * owner + 1 - xh].astype(jnp.bfloat16)
        return carry

    lax.fori_loop(0, N_Z, store, 0)


def wide_sum(refs, index):
    total = refs[0][index].astype(jnp.float32)
    for ref in refs[1:]:
        total += ref[index].astype(jnp.float32)
    return total.astype(jnp.bfloat16)


def pair_kernel(mine_ref, near_low_ref, near_high_ref, sum_ref):
    half = near_low_ref.shape[0]

    def body(i, carry):
        for start, near_ref in ((0, near_low_ref), (half, near_high_ref)):
            total = mine_ref[start + i].astype(jnp.float32) + near_ref[i].astype(jnp.float32)
            sum_ref[start + i] = total.astype(jnp.bfloat16)
        return carry

    lax.fori_loop(0, half, body, 0)


def thirds_kernel(mine_ref, near_ref, own_ref, up_ref, down_ref):
    def body(i, carry):
        for third, ref in enumerate((own_ref, up_ref, down_ref)):
            ref[i] = wide_sum((mine_ref, near_ref), 4 * third + i)
        return carry

    lax.fori_loop(0, 4, body, 0)


def quarters_kernel(where_ref, own_ref, up_ref, down_ref, *quarter_refs):
    quarter = where_ref[5] // 3
    for i, ref in enumerate(quarter_refs):
        ref[...] = wide_sum((own_ref, up_ref, down_ref), lax.rem(quarter + i, 4))


def update_kernel(mass_ref, resid_ref, projector_ref, *refs):
    update_ref, sums_ref = refs[-2:]
    resid = resid_ref[...].astype(jnp.float32)
    full = mass_ref[...] * resid
    for parts_ref in refs[:-2]:
        if len(parts_ref.shape) == 2:
            full += parts_ref[...].astype(jnp.float32)
        else:
            add = lambda i, total, ref=parts_ref: total + ref[i].astype(jnp.float32)
            full = lax.fori_loop(0, parts_ref.shape[0], add, full)
    update = full - jnp.dot(
        full, projector_ref[...], precision=EXACT, preferred_element_type=jnp.float32
    )
    update_ref[...] = update
    sums_ref[0:1, :] = jnp.sum(update * resid, axis=0, keepdims=True)
    sums_ref[1:2, :] = jnp.sum(update * update, axis=0, keepdims=True)


def shape(dims, dtype=jnp.bfloat16):
    return jax.ShapeDtypeStruct(dims, dtype)


def on_device(kernel, out_shape, scalars, *operands, scratch=(), cost=None, scalars_out=0, mib=6):
    count = len(out_shape)
    return pl.pallas_call(
        kernel,
        out_shape=out_shape,
        in_specs=[SMEM] * len(scalars) + [VMEM] * len(operands),
        out_specs=(VMEM,) * (count - scalars_out) + (SMEM,) * scalars_out,
        scratch_shapes=scratch,
        cost_estimate=cost,
        compiler_params=pltpu.CompilerParams(vmem_limit_bytes=mib * MIB),
    )(*scalars, *operands)


def after(array, *earlier):
    return pl.pallas_call(
        lambda *refs: None,
        out_shape=shape(array.shape, array.dtype),
        in_specs=[pl.BlockSpec(memory_space=pl.ANY)] * (1 + len(earlier)),
        out_specs=pl.BlockSpec(memory_space=pl.ANY),
        input_output_aliases={0: 0},
        compiler_params=pltpu.CompilerParams(vmem_limit_bytes=MIB),
    )(array, *earlier)


def step(parts, mass_rows, resid, projector):
    return on_device(
        update_kernel,
        (shape(resid.shape, jnp.float32), shape((2, resid.shape[1]), jnp.float32)),
        (),
        mass_rows,
        resid,
        projector,
        *parts,
    )


def turned(array, axis, by):
    size = lax.axis_size(axis)
    return lax.ppermute(array, axis, [((i + by) % size, i) for i in range(size)])


def gather(tile, axes, count):
    copies = jnp.broadcast_to(tile, (count,) + tile.shape[1:])
    return lax.all_to_all(copies, axes, 0, 0, tiled=True)


def final_kernel(
    sums_ref,
    p_now_ref,
    res_p_ref,
    update_p_ref,
    rt_now_ref,
    res_r_ref,
    update_r_ref,
    p_next_ref,
    res_p_next_ref,
    rt_next_ref,
    res_r_next_ref,
):
    sums = jnp.sum(sums_ref[...], axis=0)
    alpha_p = sums[0:1, 0:1] / (sums[0:1, 1:2] + EPSILON)
    alpha_r = sums[0:1, 2:3] / (sums[0:1, 3:4] + EPSILON)
    for alpha, now_ref, res_ref, update_ref, next_ref, res_next_ref in (
        (alpha_p, p_now_ref, res_p_ref, update_p_ref, p_next_ref, res_p_next_ref),
        (alpha_r, rt_now_ref, res_r_ref, update_r_ref, rt_next_ref, res_r_next_ref),
    ):
        resid = res_ref[...].astype(jnp.float32)
        next_ref[...] = (now_ref[...].astype(jnp.float32) + alpha * resid).astype(jnp.bfloat16)
        res_next_ref[...] = (resid - alpha * update_ref[...]).astype(jnp.bfloat16)


def shards(
    a_vals, a_place, a_count, p_cols, r_cols, null_layout, mass, p_now, res_p, rt_now, res_r
):
    z, xh, y, xl, core = (lax.axis_index(name) for name in AXES)
    row_id = z * N_XH + xh
    col_id = (y * N_XL + xl) * N_CORE + core
    where = jnp.stack([a_count[0, 0], xh, core, row_id, col_id, z]).astype(jnp.int32)
    tile_vals = a_vals[0, 0]
    place = a_place[0, 0].reshape(-1)
    height, width = res_p.shape[1:]
    p_flat, r_flat = p_cols.reshape(-1), r_cols.reshape(-1)
    tile = shape((height, width))
    tile_scratch = pltpu.VMEM((height, width), jnp.bfloat16)

    r_own = gather(res_r, ("y", "xl"), HALF_COL)
    own = jnp.concatenate([res_p] + [turned(res_p, "z", by) for by in (3, 6, 9)])
    thirds = (own, turned(own, "z", 1), turned(own, "z", -1))
    near = tuple(turned(third, "xh", 1) for third in thirds)
    r_own = after(r_own, *thirds[1:])
    r_other = turned(r_own, "core", 1)

    r_mine, r_theirs, where_then = on_device(
        restrict_kernel,
        (shape((N_Z, height, width)),) * 2 + (shape(where.shape, jnp.int32),),
        (where, place, r_flat),
        tile_vals,
        r_own,
        r_other,
        scratch=[pltpu.VMEM((N_ROW, height, width), jnp.float32), tile_scratch],
        cost=COST,
        mib=18,
        scalars_out=1,
    )
    r_near = turned(r_theirs, "xh", 1)
    p_mine, p_low, p_high = on_device(
        prolong_kernel,
        (shape((HALF_COL, height, width)),) + (shape((HALF_COL // 2, height, width)),) * 2,
        (where_then, place, p_flat),
        tile_vals,
        *thirds,
        *near,
        scratch=[pltpu.VMEM((N_COL, height, width), jnp.float32), tile_scratch],
        cost=COST,
        mib=18,
    )
    p_near = (turned(p_low, "core", 1), turned(p_high, "core", 1))

    r_thirds = on_device(thirds_kernel, (shape((4, height, width)),) * 3, (), r_mine, r_near)
    r_quarters = on_device(
        quarters_kernel,
        (tile,) * 4,
        (where,),
        r_thirds[0],
        turned(r_thirds[1], "z", -1),
        turned(r_thirds[2], "z", 1),
    )
    r_parts = [r_quarters[0]]
    r_parts += [turned(r_quarters[i], "z", -3 * i) for i in (1, 2, 3)]
    p_mine = after(p_mine, r_thirds[0])
    (p_sum,) = on_device(pair_kernel, (shape((HALF_COL, height, width)),), (), p_mine, *p_near)
    p_parts = [lax.all_to_all(p_sum, ("y", "xl"), 0, 0, tiled=True)]

    component = jnp.tile(null_layout % NS, width // null_layout.shape[0])
    projector = (component[:, None] == component[None, :]).astype(jnp.float32) * (NS / width)
    mass_rows = mass[0][:, None]
    update_p, sums_p = step(p_parts, mass_rows, res_p[0], projector)
    update_r, sums_r = step(r_parts, mass_rows, res_r[0], projector)
    sums = jnp.sum(jnp.concatenate([sums_p, sums_r]), axis=1)
    sums = jnp.pad(sums[None, None], ((0, 0), (0, 0), (0, width - sums.shape[0])))
    sums = gather(sums, ("xh", "xl", "core"), N_XH * N_XL * N_CORE)
    sums = gather(jnp.sum(sums, axis=0, keepdims=True), ("z", "y"), N_Z * N_Y)
    outs = on_device(
        final_kernel,
        (tile,) * 4,
        (),
        sums,
        p_now[0],
        res_p[0],
        update_p,
        rt_now[0],
        res_r[0],
        update_r,
    )
    return tuple(out[None] for out in outs)


def solution(mesh):
    fine = Mesh(mesh.devices.reshape(SIZES), AXES)
    row, col = ("z", "xh"), ("y", "xl", "core")
    tiles = P(row + col, None, None)
    in_specs = (
        P(row, col, None, None, None),
        P(row, col, None, None),
        P(row, col),
        P(),
        P(),
        P(),
        P(row + col, None),
        tiles,
        tiles,
        tiles,
        tiles,
    )
    return jax.shard_map(
        shards, mesh=fine, in_specs=in_specs, out_specs=(tiles,) * 4, check_vma=False
    )
```

```python
import functools

import jax
import jax.numpy as jnp
from jax import lax
from jax.experimental import pallas as pl
from jax.experimental.pallas import tpu as pltpu
from jax.sharding import Mesh
from jax.sharding import PartitionSpec as P

NS = 4
EPSILON = 1e-06
EXACT = lax.Precision.HIGHEST

SIZES = (12, 2, 8, 2, 2)
AXES = ("z", "xh", "y", "xl", "core")
N_Z, N_XH, N_Y, N_XL, N_CORE = SIZES
N_ROW, N_COL = N_Z * N_XH, N_Y * N_XL * N_CORE
HALF_COL = N_COL // 2
SWAP = ((0, 1), (1, 0))

VMEM = pl.BlockSpec(memory_space=pltpu.VMEM)
HBM = pl.BlockSpec(memory_space=pltpu.HBM)
SMEM = pl.BlockSpec(memory_space=pltpu.SMEM)
COST = pl.CostEstimate(flops=2**29, bytes_accessed=12 * 2**20, transcendentals=0)
MIB = 2**20


def pick_columns(tile, straight, crossed):
    block = tile.shape[1] // 2
    lane = lax.broadcasted_iota(jnp.int32, tile.shape, 1)
    left = lane < block
    wide = tile.astype(jnp.float32)
    turned = pltpu.roll(wide, block, 1)
    as_is = jnp.where(left, straight[0], straight[1]) != 0
    other = jnp.where(left, crossed[0], crossed[1]) != 0
    picked = jnp.where(as_is, wide, jnp.where(other, turned, 0.0))
    return picked.astype(jnp.bfloat16)


def matches(cols_ref, source, target):
    s0, s1 = cols_ref[2 * source], cols_ref[2 * source + 1]
    t0, t1 = cols_ref[2 * target], cols_ref[2 * target + 1]
    flag = lambda same: same.astype(jnp.int32)
    return (flag(s0 == t0), flag(s1 == t1)), (flag(s1 == t0), flag(s0 == t1))


def clear(acc_ref):
    def body(i, carry):
        acc_ref[i] = jnp.zeros(acc_ref.shape[1:], acc_ref.dtype)
        return carry

    lax.fori_loop(0, acc_ref.shape[0], body, 0)


def each_match(where_ref, place_ref, cols_ref, a_ref, turn, choose, scratch, product):
    acc_ref, held_ref, tiles_ref, held_sems, tile_sems = scratch
    count, row_id, col_id = where_ref[0], where_ref[3], where_ref[4]
    slots = a_ref.shape[0]
    hold = lambda a: pltpu.make_async_copy(a_ref.at[a], held_ref.at[a], held_sems.at[a])
    take = lambda a, ref, index: pltpu.make_async_copy(
        ref.at[index], tiles_ref.at[a], tile_sems.at[a]
    )

    def each(act):
        def body(a, carry):
            local_row, local_col = place_ref[a], place_ref[slots + a]
            tile_row = row_id * N_COL + local_row
            tile_col = local_col * N_COL + col_id
            source, target = (tile_row, tile_col) if turn else (tile_col, tile_row)
            straight, crossed = matches(cols_ref, source, target)

            @pl.when(straight[0] + straight[1] + crossed[0] + crossed[1] > 0)
            def _():
                act(a, local_row, local_col, straight, crossed)

            return carry

        lax.fori_loop(0, count, body, 0)

    def start(a, local_row, local_col, straight, crossed):
        hold(a).start()
        here, own_ref, other_ref, index = choose(local_row, local_col)

        @pl.when(here)
        def _():
            take(a, own_ref, index).start()

        @pl.when(jnp.logical_not(here))
        def _():
            take(a, other_ref, index).start()

    def finish(a, local_row, local_col, straight, crossed):
        here, own_ref, other_ref, index = choose(local_row, local_col)
        take(a, own_ref, index).wait()
        picked = pick_columns(tiles_ref[a], straight, crossed)
        hold(a).wait()
        product(held_ref[a], picked, local_row, local_col)

    each(start)
    clear(acc_ref)
    each(finish)


def prolong_kernel(
    where_ref,
    place_ref,
    cols_ref,
    own_ref,
    other_ref,
    a_ref,
    mine_ref,
    theirs_low_ref,
    theirs_high_ref,
    *scratch,
):
    xh, core = where_ref[1], where_ref[2]
    acc_ref = scratch[0]

    def choose(local_row, local_col):
        return lax.rem(local_col, N_XH) == xh, own_ref, other_ref, local_col // N_XH

    def product(block, picked, local_row, local_col):
        acc_ref[local_row] += jnp.dot(block, picked, preferred_element_type=jnp.float32)

    each_match(where_ref, place_ref, cols_ref, a_ref, False, choose, scratch, product)

    def store(q, carry):
        mine_ref[q] = acc_ref[2 * q + core].astype(jnp.bfloat16)
        return carry

    lax.fori_loop(0, HALF_COL, store, 0)

    def store_theirs(q, carry):
        theirs_low_ref[q] = acc_ref[2 * q + 1 - core].astype(jnp.bfloat16)
        theirs_high_ref[q] = acc_ref[HALF_COL + 2 * q + 1 - core].astype(jnp.bfloat16)
        return carry

    lax.fori_loop(0, HALF_COL // 2, store_theirs, 0)


def restrict_kernel(
    where_ref,
    place_ref,
    cols_ref,
    own_ref,
    other_ref,
    a_ref,
    mine_ref,
    theirs_ref,
    after_ref,
    *scratch,
):
    for i in range(where_ref.shape[0]):
        after_ref[i] = where_ref[i]
    xh, core, z = where_ref[1], where_ref[2], where_ref[5]
    acc_ref = scratch[0]

    def choose(local_row, local_col):
        return lax.rem(local_row, N_CORE) == core, own_ref, other_ref, local_row // N_CORE

    def product(block, picked, local_row, local_col):
        acc_ref[local_col] += lax.dot_general(
            block, picked, (((0,), (0,)), ((), ())), preferred_element_type=jnp.float32
        )

    each_match(where_ref, place_ref, cols_ref, a_ref, True, choose, scratch, product)

    def store(q, carry):
        owner = 3 * lax.rem(q, 4) + lax.rem(z + q // 4, 3)
        mine_ref[q] = acc_ref[2 * owner + xh].astype(jnp.bfloat16)
        theirs_ref[q] = acc_ref[2 * owner + 1 - xh].astype(jnp.bfloat16)
        return carry

    lax.fori_loop(0, N_Z, store, 0)


def wide_sum(refs, index):
    total = refs[0][index].astype(jnp.float32)
    for ref in refs[1:]:
        total += ref[index].astype(jnp.float32)
    return total.astype(jnp.bfloat16)


def pair_kernel(mine_ref, near_low_ref, near_high_ref, sum_ref):
    half = near_low_ref.shape[0]

    def body(i, carry):
        for start, near_ref in ((0, near_low_ref), (half, near_high_ref)):
            total = mine_ref[start + i].astype(jnp.float32) + near_ref[i].astype(jnp.float32)
            sum_ref[start + i] = total.astype(jnp.bfloat16)
        return carry

    lax.fori_loop(0, half, body, 0)


def thirds_kernel(mine_ref, near_ref, own_ref, up_ref, down_ref):
    def body(i, carry):
        for third, ref in enumerate((own_ref, up_ref, down_ref)):
            ref[i] = wide_sum((mine_ref, near_ref), 4 * third + i)
        return carry

    lax.fori_loop(0, 4, body, 0)


def quarters_kernel(where_ref, own_ref, up_ref, down_ref, *quarter_refs):
    quarter = where_ref[5] // 3
    for i, ref in enumerate(quarter_refs):
        ref[...] = wide_sum((own_ref, up_ref, down_ref), lax.rem(quarter + i, 4))


def update_kernel(mass_ref, resid_ref, projector_ref, *refs):
    update_ref, sums_ref = refs[-2:]
    resid = resid_ref[...].astype(jnp.float32)
    full = mass_ref[...] * resid
    for parts_ref in refs[:-2]:
        if len(parts_ref.shape) == 2:
            full += parts_ref[...].astype(jnp.float32)
        else:
            add = lambda i, total, ref=parts_ref: total + ref[i].astype(jnp.float32)
            full = lax.fori_loop(0, parts_ref.shape[0], add, full)
    update = full - jnp.dot(
        full, projector_ref[...], precision=EXACT, preferred_element_type=jnp.float32
    )
    update_ref[...] = update
    sums_ref[0:1, :] = jnp.sum(update * resid, axis=0, keepdims=True)
    sums_ref[1:2, :] = jnp.sum(update * update, axis=0, keepdims=True)


def shape(dims, dtype=jnp.bfloat16):
    return jax.ShapeDtypeStruct(dims, dtype)


def on_device(
    kernel, out_shape, scalars, *operands, left=(), scratch=(), cost=None, scalars_out=0, mib=6
):
    count = len(out_shape)
    return pl.pallas_call(
        kernel,
        out_shape=out_shape,
        in_specs=[SMEM] * len(scalars) + [VMEM] * len(operands) + [HBM] * len(left),
        out_specs=(VMEM,) * (count - scalars_out) + (SMEM,) * scalars_out,
        scratch_shapes=scratch,
        cost_estimate=cost,
        compiler_params=pltpu.CompilerParams(vmem_limit_bytes=mib * MIB),
    )(*scalars, *operands, *left)


def after(array, *earlier):
    return pl.pallas_call(
        lambda *refs: None,
        out_shape=shape(array.shape, array.dtype),
        in_specs=[pl.BlockSpec(memory_space=pl.ANY)] * (1 + len(earlier)),
        out_specs=pl.BlockSpec(memory_space=pl.ANY),
        input_output_aliases={0: 0},
        compiler_params=pltpu.CompilerParams(vmem_limit_bytes=MIB),
    )(array, *earlier)


def step(parts, mass_rows, resid, projector):
    return on_device(
        update_kernel,
        (shape(resid.shape, jnp.float32), shape((2, resid.shape[1]), jnp.float32)),
        (),
        mass_rows,
        resid,
        projector,
        *parts,
    )


def turned(array, axis, by):
    size = lax.axis_size(axis)
    return lax.ppermute(array, axis, [((i + by) % size, i) for i in range(size)])


def gather(tile, axes, count):
    copies = jnp.broadcast_to(tile, (count,) + tile.shape[1:])
    return lax.all_to_all(copies, axes, 0, 0, tiled=True)


def final_kernel(
    sums_ref,
    p_now_ref,
    res_p_ref,
    update_p_ref,
    rt_now_ref,
    res_r_ref,
    update_r_ref,
    p_next_ref,
    res_p_next_ref,
    rt_next_ref,
    res_r_next_ref,
):
    sums = jnp.sum(sums_ref[...], axis=0)
    alpha_p = sums[0:1, 0:1] / (sums[0:1, 1:2] + EPSILON)
    alpha_r = sums[0:1, 2:3] / (sums[0:1, 3:4] + EPSILON)
    for alpha, now_ref, res_ref, update_ref, next_ref, res_next_ref in (
        (alpha_p, p_now_ref, res_p_ref, update_p_ref, p_next_ref, res_p_next_ref),
        (alpha_r, rt_now_ref, res_r_ref, update_r_ref, rt_next_ref, res_r_next_ref),
    ):
        resid = res_ref[...].astype(jnp.float32)
        next_ref[...] = (now_ref[...].astype(jnp.float32) + alpha * resid).astype(jnp.bfloat16)
        res_next_ref[...] = (resid - alpha * update_ref[...]).astype(jnp.bfloat16)


def shards(
    a_vals, a_place, a_count, p_cols, r_cols, null_layout, mass, p_now, res_p, rt_now, res_r
):
    z, xh, y, xl, core = (lax.axis_index(name) for name in AXES)
    row_id = z * N_XH + xh
    col_id = (y * N_XL + xl) * N_CORE + core
    where = jnp.stack([a_count[0, 0], xh, core, row_id, col_id, z]).astype(jnp.int32)
    tile_vals = a_vals[0, 0]
    place = a_place[0, 0].reshape(-1)
    height, width = res_p.shape[1:]
    p_flat, r_flat = p_cols.reshape(-1), r_cols.reshape(-1)
    tile = shape((height, width))
    slots = tile_vals.shape[0]
    scratch = (
        pltpu.VMEM(tile_vals.shape, jnp.bfloat16),
        pltpu.VMEM((slots, height, width), jnp.bfloat16),
        pltpu.SemaphoreType.DMA((slots,)),
        pltpu.SemaphoreType.DMA((slots,)),
    )

    r_own = gather(res_r, ("y", "xl"), HALF_COL)
    p_own = lax.all_gather(res_p, "z", axis=0, tiled=True)
    p_other = turned(p_own, "xh", 1)
    r_own = after(r_own, p_own)
    r_other = turned(r_own, "core", 1)

    r_mine, r_theirs, where_then = on_device(
        restrict_kernel,
        (shape((N_Z, height, width)),) * 2 + (shape(where.shape, jnp.int32),),
        (where, place, r_flat),
        left=(r_own, r_other, tile_vals),
        scratch=[pltpu.VMEM((N_ROW, height, width), jnp.float32), *scratch],
        cost=COST,
        mib=48,
        scalars_out=1,
    )
    r_near = turned(r_theirs, "xh", 1)
    p_mine, p_low, p_high = on_device(
        prolong_kernel,
        (shape((HALF_COL, height, width)),) + (shape((HALF_COL // 2, height, width)),) * 2,
        (where_then, place, p_flat),
        left=(p_own, p_other, tile_vals),
        scratch=[pltpu.VMEM((N_COL, height, width), jnp.float32), *scratch],
        cost=COST,
        mib=48,
    )
    p_near = (turned(p_low, "core", 1), turned(p_high, "core", 1))

    r_thirds = on_device(thirds_kernel, (shape((4, height, width)),) * 3, (), r_mine, r_near)
    r_quarters = on_device(
        quarters_kernel,
        (tile,) * 4,
        (where,),
        r_thirds[0],
        turned(r_thirds[1], "z", -1),
        turned(r_thirds[2], "z", 1),
    )
    r_parts = [r_quarters[0]]
    r_parts += [turned(r_quarters[i], "z", -3 * i) for i in (1, 2, 3)]
    p_mine = after(p_mine, r_thirds[0])
    (p_sum,) = on_device(pair_kernel, (shape((HALF_COL, height, width)),), (), p_mine, *p_near)
    p_parts = [lax.all_to_all(p_sum, ("y", "xl"), 0, 0, tiled=True)]

    component = jnp.tile(null_layout % NS, width // null_layout.shape[0])
    projector = (component[:, None] == component[None, :]).astype(jnp.float32) * (NS / width)
    mass_rows = mass[0][:, None]
    update_p, sums_p = step(p_parts, mass_rows, res_p[0], projector)
    update_r, sums_r = step(r_parts, mass_rows, res_r[0], projector)
    sums = jnp.sum(jnp.concatenate([sums_p, sums_r]), axis=1)
    sums = jnp.pad(sums[None, None], ((0, 0), (0, 0), (0, width - sums.shape[0])))
    sums = gather(sums, ("xh", "xl", "core"), N_XH * N_XL * N_CORE)
    sums = gather(jnp.sum(sums, axis=0, keepdims=True), ("z", "y"), N_Z * N_Y)
    outs = on_device(
        final_kernel,
        (tile,) * 4,
        (),
        sums,
        p_now[0],
        res_p[0],
        update_p,
        rt_now[0],
        res_r[0],
        update_r,
    )
    return tuple(out[None] for out in outs)


def solution(mesh):
    fine = Mesh(mesh.devices.reshape(SIZES), AXES)
    row, col = ("z", "xh"), ("y", "xl", "core")
    tiles = P(row + col, None, None)
    in_specs = (
        P(row, col, None, None, None),
        P(row, col, None, None),
        P(row, col),
        P(),
        P(),
        P(),
        P(row + col, None),
        tiles,
        tiles,
        tiles,
        tiles,
    )
    return jax.shard_map(
        shards, mesh=fine, in_specs=in_specs, out_specs=(tiles,) * 4, check_vma=False
    )
```

```python
import functools

import jax
import jax.numpy as jnp
from jax import lax
from jax.experimental import pallas as pl
from jax.experimental.pallas import tpu as pltpu
from jax.sharding import Mesh
from jax.sharding import PartitionSpec as P

NS = 4
EPSILON = 1e-06
EXACT = lax.Precision.HIGHEST

SIZES = (12, 2, 8, 2, 2)
AXES = ("z", "xh", "y", "xl", "core")
N_Z, N_XH, N_Y, N_XL, N_CORE = SIZES
N_ROW, N_COL = N_Z * N_XH, N_Y * N_XL * N_CORE
HALF_COL = N_COL // 2
SWAP = ((0, 1), (1, 0))

VMEM = pl.BlockSpec(memory_space=pltpu.VMEM)
HBM = pl.BlockSpec(memory_space=pltpu.HBM)
SMEM = pl.BlockSpec(memory_space=pltpu.SMEM)
COST = pl.CostEstimate(flops=2**29, bytes_accessed=12 * 2**20, transcendentals=0)
MIB = 2**20


def add_columns(acc_ref, index, whole, straight, crossed):
    block = whole.shape[1] // 2
    left = lax.broadcasted_iota(jnp.int32, (1, whole.shape[1]), 1) < block

    @pl.when(straight[0] + straight[1] > 0)
    def _():
        keep = jnp.where(left, straight[0], straight[1]) != 0
        acc_ref[index] += jnp.where(keep, whole, 0.0)

    @pl.when(crossed[0] + crossed[1] > 0)
    def _():
        keep = jnp.where(left, crossed[0], crossed[1]) != 0
        acc_ref[index] += jnp.where(keep, pltpu.roll(whole, block, 1), 0.0)


def matches(cols_ref, source, target):
    s0, s1 = cols_ref[2 * source], cols_ref[2 * source + 1]
    t0, t1 = cols_ref[2 * target], cols_ref[2 * target + 1]
    flag = lambda same: same.astype(jnp.int32)
    return (flag(s0 == t0), flag(s1 == t1)), (flag(s1 == t0), flag(s0 == t1))


def clear(acc_ref):
    def body(i, carry):
        acc_ref[i] = jnp.zeros(acc_ref.shape[1:], acc_ref.dtype)
        return carry

    lax.fori_loop(0, acc_ref.shape[0], body, 0)


def each_match(where_ref, place_ref, cols_ref, a_ref, turn, choose, scratch, product):
    acc_ref, held_ref, tiles_ref, held_sems, tile_sems = scratch
    count, row_id, col_id = where_ref[0], where_ref[3], where_ref[4]
    slots = a_ref.shape[0]
    hold = lambda a: pltpu.make_async_copy(a_ref.at[a], held_ref.at[a], held_sems.at[a])
    take = lambda a, ref, index: pltpu.make_async_copy(
        ref.at[index], tiles_ref.at[a], tile_sems.at[a]
    )

    def each(act):
        def body(a, carry):
            local_row, local_col = place_ref[a], place_ref[slots + a]
            tile_row = row_id * N_COL + local_row
            tile_col = local_col * N_COL + col_id
            source, target = (tile_row, tile_col) if turn else (tile_col, tile_row)
            straight, crossed = matches(cols_ref, source, target)

            @pl.when(straight[0] + straight[1] + crossed[0] + crossed[1] > 0)
            def _():
                act(a, local_row, local_col, straight, crossed)

            return carry

        lax.fori_loop(0, count, body, 0)

    def start(a, local_row, local_col, straight, crossed):
        hold(a).start()
        here, own_ref, other_ref, index = choose(local_row, local_col)

        @pl.when(here)
        def _():
            take(a, own_ref, index).start()

        @pl.when(jnp.logical_not(here))
        def _():
            take(a, other_ref, index).start()

    def finish(a, local_row, local_col, straight, crossed):
        here, own_ref, other_ref, index = choose(local_row, local_col)
        take(a, own_ref, index).wait()
        hold(a).wait()
        product(held_ref[a], tiles_ref[a], local_row, local_col, straight, crossed)

    each(start)
    clear(acc_ref)
    each(finish)


def prolong_kernel(
    where_ref,
    place_ref,
    cols_ref,
    own_ref,
    other_ref,
    a_ref,
    mine_ref,
    theirs_low_ref,
    theirs_high_ref,
    *scratch,
):
    xh, core = where_ref[1], where_ref[2]
    acc_ref = scratch[0]

    def choose(local_row, local_col):
        return lax.rem(local_col, N_XH) == xh, own_ref, other_ref, local_col // N_XH

    def product(block, tile, local_row, local_col, straight, crossed):
        whole = jnp.dot(block, tile, preferred_element_type=jnp.float32)
        add_columns(acc_ref, local_row, whole, straight, crossed)

    each_match(where_ref, place_ref, cols_ref, a_ref, False, choose, scratch, product)

    def store(q, carry):
        mine_ref[q] = acc_ref[2 * q + core].astype(jnp.bfloat16)
        return carry

    lax.fori_loop(0, HALF_COL, store, 0)

    def store_theirs(q, carry):
        theirs_low_ref[q] = acc_ref[2 * q + 1 - core].astype(jnp.bfloat16)
        theirs_high_ref[q] = acc_ref[HALF_COL + 2 * q + 1 - core].astype(jnp.bfloat16)
        return carry

    lax.fori_loop(0, HALF_COL // 2, store_theirs, 0)


def restrict_kernel(
    where_ref,
    place_ref,
    cols_ref,
    own_ref,
    other_ref,
    a_ref,
    own_third_ref,
    up_third_ref,
    down_third_ref,
    after_ref,
    *scratch,
):
    for i in range(where_ref.shape[0]):
        after_ref[i] = where_ref[i]
    core, z = where_ref[2], where_ref[5]
    acc_ref = scratch[0]

    def choose(local_row, local_col):
        return lax.rem(local_row, N_CORE) == core, own_ref, other_ref, local_row // N_CORE

    def product(block, tile, local_row, local_col, straight, crossed):
        whole = lax.dot_general(
            block, tile, (((0,), (0,)), ((), ())), preferred_element_type=jnp.float32
        )
        add_columns(acc_ref, local_col, whole, straight, crossed)

    each_match(where_ref, place_ref, cols_ref, a_ref, True, choose, scratch, product)

    def store(q, carry):
        for third, ref in enumerate((own_third_ref, up_third_ref, down_third_ref)):
            owner = 3 * (q // N_XH) + lax.rem(z + third, 3)
            ref[q] = acc_ref[N_XH * owner + lax.rem(q, N_XH)].astype(jnp.bfloat16)
        return carry

    lax.fori_loop(0, N_ROW // 3, store, 0)


def wide_sum(refs, index):
    total = refs[0][index].astype(jnp.float32)
    for ref in refs[1:]:
        total += ref[index].astype(jnp.float32)
    return total.astype(jnp.bfloat16)


def pair_kernel(mine_ref, near_low_ref, near_high_ref, sum_ref):
    half = near_low_ref.shape[0]

    def body(i, carry):
        for start, near_ref in ((0, near_low_ref), (half, near_high_ref)):
            total = mine_ref[start + i].astype(jnp.float32) + near_ref[i].astype(jnp.float32)
            sum_ref[start + i] = total.astype(jnp.bfloat16)
        return carry

    lax.fori_loop(0, half, body, 0)


def quarters_kernel(where_ref, own_ref, up_ref, down_ref, *quarter_refs):
    quarter = where_ref[5] // 3
    for i, ref in enumerate(quarter_refs):
        for x in range(N_XH):
            index = N_XH * lax.rem(quarter + i, 4) + x
            ref[x] = wide_sum((own_ref, up_ref, down_ref), index)


def halves_kernel(where_ref, *refs):
    quarter_refs, (mine_ref, theirs_ref) = refs[:-2], refs[-2:]
    xh = where_ref[1]
    mine_ref[...] = wide_sum(quarter_refs, xh)
    theirs_ref[...] = wide_sum(quarter_refs, 1 - xh)


def update_kernel(mass_ref, resid_ref, projector_ref, *refs):
    update_ref, sums_ref = refs[-2:]
    resid = resid_ref[...].astype(jnp.float32)
    full = mass_ref[...] * resid
    for parts_ref in refs[:-2]:
        if len(parts_ref.shape) == 2:
            full += parts_ref[...].astype(jnp.float32)
        else:
            add = lambda i, total, ref=parts_ref: total + ref[i].astype(jnp.float32)
            full = lax.fori_loop(0, parts_ref.shape[0], add, full)
    update = full - jnp.dot(
        full, projector_ref[...], precision=EXACT, preferred_element_type=jnp.float32
    )
    update_ref[...] = update
    sums_ref[0:1, :] = jnp.sum(update * resid, axis=0, keepdims=True)
    sums_ref[1:2, :] = jnp.sum(update * update, axis=0, keepdims=True)


def shape(dims, dtype=jnp.bfloat16):
    return jax.ShapeDtypeStruct(dims, dtype)


def on_device(
    kernel, out_shape, scalars, *operands, left=(), scratch=(), cost=None, scalars_out=0, mib=6
):
    count = len(out_shape)
    return pl.pallas_call(
        kernel,
        out_shape=out_shape,
        in_specs=[SMEM] * len(scalars) + [VMEM] * len(operands) + [HBM] * len(left),
        out_specs=(VMEM,) * (count - scalars_out) + (SMEM,) * scalars_out,
        scratch_shapes=scratch,
        cost_estimate=cost,
        compiler_params=pltpu.CompilerParams(vmem_limit_bytes=mib * MIB),
    )(*scalars, *operands, *left)


def after(array, *earlier):
    return pl.pallas_call(
        lambda *refs: None,
        out_shape=shape(array.shape, array.dtype),
        in_specs=[pl.BlockSpec(memory_space=pl.ANY)] * (1 + len(earlier)),
        out_specs=pl.BlockSpec(memory_space=pl.ANY),
        input_output_aliases={0: 0},
        compiler_params=pltpu.CompilerParams(vmem_limit_bytes=MIB),
    )(array, *earlier)


def step(parts, mass_rows, resid, projector):
    return on_device(
        update_kernel,
        (shape(resid.shape, jnp.float32), shape((2, resid.shape[1]), jnp.float32)),
        (),
        mass_rows,
        resid,
        projector,
        *parts,
    )


def turned(array, axis, by):
    size = lax.axis_size(axis)
    if by % size == 0:
        return array
    return lax.ppermute(array, axis, [((i + by) % size, i) for i in range(size)])


def gather(tile, axes, count):
    copies = jnp.broadcast_to(tile, (count,) + tile.shape[1:])
    return lax.all_to_all(copies, axes, 0, 0, tiled=True)


def final_kernel(
    sums_ref,
    p_now_ref,
    res_p_ref,
    update_p_ref,
    rt_now_ref,
    res_r_ref,
    update_r_ref,
    p_next_ref,
    res_p_next_ref,
    rt_next_ref,
    res_r_next_ref,
):
    sums = jnp.sum(sums_ref[...], axis=0)
    alpha_p = sums[0:1, 0:1] / (sums[0:1, 1:2] + EPSILON)
    alpha_r = sums[0:1, 2:3] / (sums[0:1, 3:4] + EPSILON)
    for alpha, now_ref, res_ref, update_ref, next_ref, res_next_ref in (
        (alpha_p, p_now_ref, res_p_ref, update_p_ref, p_next_ref, res_p_next_ref),
        (alpha_r, rt_now_ref, res_r_ref, update_r_ref, rt_next_ref, res_r_next_ref),
    ):
        resid = res_ref[...].astype(jnp.float32)
        next_ref[...] = (now_ref[...].astype(jnp.float32) + alpha * resid).astype(jnp.bfloat16)
        res_next_ref[...] = (resid - alpha * update_ref[...]).astype(jnp.bfloat16)


def shards(
    a_vals, a_place, a_count, p_cols, r_cols, null_layout, mass, p_now, res_p, rt_now, res_r
):
    z, xh, y, xl, core = (lax.axis_index(name) for name in AXES)
    row_id = z * N_XH + xh
    col_id = (y * N_XL + xl) * N_CORE + core
    where = jnp.stack([a_count[0, 0], xh, core, row_id, col_id, z]).astype(jnp.int32)
    tile_vals = a_vals[0, 0]
    place = a_place[0, 0].reshape(-1)
    height, width = res_p.shape[1:]
    p_flat, r_flat = p_cols.reshape(-1), r_cols.reshape(-1)
    tile = shape((height, width))
    slots = tile_vals.shape[0]
    scratch = (
        pltpu.VMEM(tile_vals.shape, jnp.bfloat16),
        pltpu.VMEM((slots, height, width), jnp.bfloat16),
        pltpu.SemaphoreType.DMA((slots,)),
        pltpu.SemaphoreType.DMA((slots,)),
    )

    r_own = gather(res_r, ("y", "xl"), HALF_COL)
    p_own = lax.all_gather(res_p, "z", axis=0, tiled=True)
    p_other = turned(p_own, "xh", 1)
    r_own = after(r_own, p_own)
    r_other = turned(r_own, "core", 1)

    *r_thirds, where_then = on_device(
        restrict_kernel,
        (shape((N_ROW // 3, height, width)),) * 3 + (shape(where.shape, jnp.int32),),
        (where, place, r_flat),
        left=(r_own, r_other, tile_vals),
        scratch=[pltpu.VMEM((N_ROW, height, width), jnp.float32), *scratch],
        cost=COST,
        mib=48,
        scalars_out=1,
    )
    r_thirds = (r_thirds[0], turned(r_thirds[1], "z", -1), turned(r_thirds[2], "z", 1))
    p_mine, p_low, p_high = on_device(
        prolong_kernel,
        (shape((HALF_COL, height, width)),) + (shape((HALF_COL // 2, height, width)),) * 2,
        (where_then, place, p_flat),
        left=(p_own, p_other, tile_vals),
        scratch=[pltpu.VMEM((N_COL, height, width), jnp.float32), *scratch],
        cost=COST,
        mib=48,
    )
    p_near = (turned(p_low, "core", 1), turned(p_high, "core", 1))

    r_quarters = on_device(
        quarters_kernel, (shape((N_XH, height, width)),) * 4, (where,), *r_thirds
    )
    r_quarters = [turned(quarter, "z", -3 * i) for i, quarter in enumerate(r_quarters)]
    r_mine, r_theirs = on_device(halves_kernel, (tile,) * 2, (where,), *r_quarters)
    r_parts = (r_mine, turned(r_theirs, "xh", 1))
    p_mine = after(p_mine, r_quarters[0])
    (p_sum,) = on_device(pair_kernel, (shape((HALF_COL, height, width)),), (), p_mine, *p_near)
    p_parts = [lax.all_to_all(p_sum, ("y", "xl"), 0, 0, tiled=True)]

    component = jnp.tile(null_layout % NS, width // null_layout.shape[0])
    projector = (component[:, None] == component[None, :]).astype(jnp.float32) * (NS / width)
    mass_rows = mass[0][:, None]
    update_p, sums_p = step(p_parts, mass_rows, res_p[0], projector)
    update_r, sums_r = step(r_parts, mass_rows, res_r[0], projector)
    sums = jnp.sum(jnp.concatenate([sums_p, sums_r]), axis=1)
    sums = jnp.pad(sums[None, None], ((0, 0), (0, 0), (0, width - sums.shape[0])))
    sums = gather(sums, ("xh", "xl", "core"), N_XH * N_XL * N_CORE)
    sums = gather(jnp.sum(sums, axis=0, keepdims=True), ("z", "y"), N_Z * N_Y)
    outs = on_device(
        final_kernel,
        (tile,) * 4,
        (),
        sums,
        p_now[0],
        res_p[0],
        update_p,
        rt_now[0],
        res_r[0],
        update_r,
    )
    return tuple(out[None] for out in outs)


def solution(mesh):
    fine = Mesh(mesh.devices.reshape(SIZES), AXES)
    row, col = ("z", "xh"), ("y", "xl", "core")
    tiles = P(row + col, None, None)
    in_specs = (
        P(row, col, None, None, None),
        P(row, col, None, None),
        P(row, col),
        P(),
        P(),
        P(),
        P(row + col, None),
        tiles,
        tiles,
        tiles,
        tiles,
    )
    return jax.shard_map(
        shards, mesh=fine, in_specs=in_specs, out_specs=(tiles,) * 4, check_vma=False
    )
```

```python
import functools

import jax
import jax.numpy as jnp
from jax import lax
from jax.experimental import pallas as pl
from jax.experimental.pallas import tpu as pltpu
from jax.sharding import Mesh
from jax.sharding import PartitionSpec as P

NS = 4
EPSILON = 1e-06
EXACT = lax.Precision.HIGHEST

SIZES = (12, 2, 8, 2, 2)
AXES = ("z", "xh", "y", "xl", "core")
N_Z, N_XH, N_Y, N_XL, N_CORE = SIZES
N_ROW, N_COL = N_Z * N_XH, N_Y * N_XL * N_CORE
HALF_COL = N_COL // 2
SWAP = ((0, 1), (1, 0))

VMEM = pl.BlockSpec(memory_space=pltpu.VMEM)
HBM = pl.BlockSpec(memory_space=pltpu.HBM)
SMEM = pl.BlockSpec(memory_space=pltpu.SMEM)
COST = pl.CostEstimate(flops=2**29, bytes_accessed=12 * 2**20, transcendentals=0)
MIB = 2**20


def matches(cols_ref, source, target):
    s0, s1 = cols_ref[2 * source], cols_ref[2 * source + 1]
    t0, t1 = cols_ref[2 * target], cols_ref[2 * target + 1]
    flag = lambda same, bit: jnp.where(same, bit, 0)
    return flag(s0 == t0, 1) + flag(s1 == t1, 2) + flag(s1 == t0, 4) + flag(s0 == t1, 8)


def plan_kernel(where_ref, place_ref, p_cols_ref, r_cols_ref, p_plan_ref, r_plan_ref):
    count, xh, core = where_ref[0], where_ref[1], where_ref[2]
    row_id, col_id = where_ref[3], where_ref[4]
    slots = place_ref.shape[0] // 2

    def note(plan_ref, used, slot, target, index, blocks):
        for field, value in enumerate((slot, target, index, blocks)):
            plan_ref[field * slots + used] = value
        return used + jnp.where(blocks != 0, 1, 0)

    def body(a, used):
        local_row, local_col = place_ref[a], place_ref[slots + a]
        tile_row = row_id * N_COL + local_row
        tile_col = local_col * N_COL + col_id
        p_index = local_col // N_XH + jnp.where(lax.rem(local_col, N_XH) == xh, 0, N_Z)
        r_index = local_row // N_CORE + jnp.where(lax.rem(local_row, N_CORE) == core, 0, HALF_COL)
        p_blocks = matches(p_cols_ref, tile_col, tile_row)
        r_blocks = matches(r_cols_ref, tile_row, tile_col)
        return (
            note(p_plan_ref, used[0], a, local_row, p_index, p_blocks),
            note(r_plan_ref, used[1], a, local_col, r_index, r_blocks),
        )

    p_used, r_used = lax.fori_loop(0, count, body, (0, 0))
    p_plan_ref[4 * slots] = p_used
    r_plan_ref[4 * slots] = r_used


def clear(acc_ref):
    def body(i, carry):
        acc_ref[i] = jnp.zeros(acc_ref.shape[1:], acc_ref.dtype)
        return carry

    lax.fori_loop(0, acc_ref.shape[0], body, 0)


def add_columns(acc_ref, index, whole, blocks):
    block = whole.shape[1] // 2
    left = lax.broadcasted_iota(jnp.int32, (1, whole.shape[1]), 1) < block

    @pl.when((blocks & 3) != 0)
    def _():
        keep = jnp.where(left, blocks & 1, blocks & 2) != 0
        acc_ref[index] += jnp.where(keep, whole, 0.0)

    @pl.when((blocks & 12) != 0)
    def _():
        keep = jnp.where(left, blocks & 4, blocks & 8) != 0
        acc_ref[index] += jnp.where(keep, pltpu.roll(whole, block, 1), 0.0)


def each_used(plan_ref, own_ref, other_ref, a_ref, scratch, product):
    acc_ref, held_ref, tiles_ref, held_sems, tile_sems = scratch
    slots, own_count = a_ref.shape[0], own_ref.shape[0]
    used = plan_ref[4 * slots]
    hold = lambda k: pltpu.make_async_copy(
        a_ref.at[plan_ref[k]], held_ref.at[k], held_sems.at[k]
    )
    take = lambda k, ref, index: pltpu.make_async_copy(
        ref.at[index], tiles_ref.at[k], tile_sems.at[k]
    )

    def start(k, carry):
        index = plan_ref[2 * slots + k]

        @pl.when(index < own_count)
        def _():
            take(k, own_ref, index).start()

        @pl.when(index >= own_count)
        def _():
            take(k, other_ref, index - own_count).start()

        hold(k).start()
        return carry

    def finish(k, carry):
        take(k, own_ref, 0).wait()
        hold(k).wait()
        whole = product(held_ref[k], tiles_ref[k])
        add_columns(acc_ref, plan_ref[slots + k], whole, plan_ref[3 * slots + k])
        return carry

    lax.fori_loop(0, used, start, 0)
    clear(acc_ref)
    lax.fori_loop(0, used, finish, 0)


def prolong_kernel(
    where_ref,
    plan_ref,
    own_ref,
    other_ref,
    a_ref,
    mine_ref,
    theirs_low_ref,
    theirs_high_ref,
    *scratch,
):
    core = where_ref[2]
    acc_ref = scratch[0]
    product = functools.partial(jnp.dot, preferred_element_type=jnp.float32)
    each_used(plan_ref, own_ref, other_ref, a_ref, scratch, product)

    def store(q, carry):
        mine_ref[q] = acc_ref[2 * q + core].astype(jnp.bfloat16)
        return carry

    lax.fori_loop(0, HALF_COL, store, 0)

    def store_theirs(q, carry):
        theirs_low_ref[q] = acc_ref[2 * q + 1 - core].astype(jnp.bfloat16)
        theirs_high_ref[q] = acc_ref[HALF_COL + 2 * q + 1 - core].astype(jnp.bfloat16)
        return carry

    lax.fori_loop(0, HALF_COL // 2, store_theirs, 0)


def restrict_kernel(
    where_ref,
    plan_ref,
    own_ref,
    other_ref,
    a_ref,
    own_third_ref,
    up_third_ref,
    down_third_ref,
    after_ref,
    *scratch,
):
    for i in range(where_ref.shape[0]):
        after_ref[i] = where_ref[i]
    z, acc_ref = where_ref[5], scratch[0]

    def product(block, tile):
        return lax.dot_general(
            block, tile, (((0,), (0,)), ((), ())), preferred_element_type=jnp.float32
        )

    each_used(plan_ref, own_ref, other_ref, a_ref, scratch, product)

    def store(q, carry):
        for third, ref in enumerate((own_third_ref, up_third_ref, down_third_ref)):
            owner = 3 * (q // N_XH) + lax.rem(z + third, 3)
            ref[q] = acc_ref[N_XH * owner + lax.rem(q, N_XH)].astype(jnp.bfloat16)
        return carry

    lax.fori_loop(0, N_ROW // 3, store, 0)


def wide_sum(refs, index):
    total = refs[0][index].astype(jnp.float32)
    for ref in refs[1:]:
        total += ref[index].astype(jnp.float32)
    return total.astype(jnp.bfloat16)


def pair_kernel(mine_ref, near_low_ref, near_high_ref, sum_ref):
    half = near_low_ref.shape[0]

    def body(i, carry):
        for start, near_ref in ((0, near_low_ref), (half, near_high_ref)):
            total = mine_ref[start + i].astype(jnp.float32) + near_ref[i].astype(jnp.float32)
            sum_ref[start + i] = total.astype(jnp.bfloat16)
        return carry

    lax.fori_loop(0, half, body, 0)


def thirds_kernel(where_ref, own_ref, up_ref, down_ref, mine_ref, theirs_ref):
    quarter, xh = where_ref[5] // 3, where_ref[1]
    for i in range(mine_ref.shape[0]):
        index = N_XH * lax.rem(quarter + i, 4)
        mine_ref[i] = wide_sum((own_ref, up_ref, down_ref), index + xh)
        theirs_ref[i] = wide_sum((own_ref, up_ref, down_ref), index + 1 - xh)


def halves_kernel(mine_ref, near_ref, *quarter_refs):
    for i, ref in enumerate(quarter_refs):
        ref[...] = wide_sum((mine_ref, near_ref), i)


def update_kernel(mass_ref, resid_ref, projector_ref, *refs):
    update_ref, sums_ref = refs[-2:]
    resid = resid_ref[...].astype(jnp.float32)
    full = mass_ref[...] * resid
    for parts_ref in refs[:-2]:
        if len(parts_ref.shape) == 2:
            full += parts_ref[...].astype(jnp.float32)
        else:
            add = lambda i, total, ref=parts_ref: total + ref[i].astype(jnp.float32)
            full = lax.fori_loop(0, parts_ref.shape[0], add, full)
    update = full - jnp.dot(
        full, projector_ref[...], precision=EXACT, preferred_element_type=jnp.float32
    )
    update_ref[...] = update
    sums_ref[0:1, :] = jnp.sum(update * resid, axis=0, keepdims=True)
    sums_ref[1:2, :] = jnp.sum(update * update, axis=0, keepdims=True)


def shape(dims, dtype=jnp.bfloat16):
    return jax.ShapeDtypeStruct(dims, dtype)


def on_device(
    kernel, out_shape, scalars, *operands, left=(), scratch=(), cost=None, scalars_out=0, mib=6
):
    count = len(out_shape)
    return pl.pallas_call(
        kernel,
        out_shape=out_shape,
        in_specs=[SMEM] * len(scalars) + [VMEM] * len(operands) + [HBM] * len(left),
        out_specs=(VMEM,) * (count - scalars_out) + (SMEM,) * scalars_out,
        scratch_shapes=scratch,
        cost_estimate=cost,
        compiler_params=pltpu.CompilerParams(vmem_limit_bytes=mib * MIB),
    )(*scalars, *operands, *left)


def after(array, *earlier):
    return pl.pallas_call(
        lambda *refs: None,
        out_shape=shape(array.shape, array.dtype),
        in_specs=[pl.BlockSpec(memory_space=pl.ANY)] * (1 + len(earlier)),
        out_specs=pl.BlockSpec(memory_space=pl.ANY),
        input_output_aliases={0: 0},
        compiler_params=pltpu.CompilerParams(vmem_limit_bytes=MIB),
    )(array, *earlier)


def step(parts, mass_rows, resid, projector):
    return on_device(
        update_kernel,
        (shape(resid.shape, jnp.float32), shape((2, resid.shape[1]), jnp.float32)),
        (),
        mass_rows,
        resid,
        projector,
        *parts,
    )


def turned(array, axis, by):
    size = lax.axis_size(axis)
    if by % size == 0:
        return array
    return lax.ppermute(array, axis, [((i + by) % size, i) for i in range(size)])


def gather(tile, axes, count):
    copies = jnp.broadcast_to(tile, (count,) + tile.shape[1:])
    return lax.all_to_all(copies, axes, 0, 0, tiled=True)


def final_kernel(
    sums_ref,
    p_now_ref,
    res_p_ref,
    update_p_ref,
    rt_now_ref,
    res_r_ref,
    update_r_ref,
    p_next_ref,
    res_p_next_ref,
    rt_next_ref,
    res_r_next_ref,
):
    sums = jnp.sum(sums_ref[...], axis=0)
    alpha_p = sums[0:1, 0:1] / (sums[0:1, 1:2] + EPSILON)
    alpha_r = sums[0:1, 2:3] / (sums[0:1, 3:4] + EPSILON)
    for alpha, now_ref, res_ref, update_ref, next_ref, res_next_ref in (
        (alpha_p, p_now_ref, res_p_ref, update_p_ref, p_next_ref, res_p_next_ref),
        (alpha_r, rt_now_ref, res_r_ref, update_r_ref, rt_next_ref, res_r_next_ref),
    ):
        resid = res_ref[...].astype(jnp.float32)
        next_ref[...] = (now_ref[...].astype(jnp.float32) + alpha * resid).astype(jnp.bfloat16)
        res_next_ref[...] = (resid - alpha * update_ref[...]).astype(jnp.bfloat16)


def shards(
    a_vals, a_place, a_count, p_cols, r_cols, null_layout, mass, p_now, res_p, rt_now, res_r
):
    z, xh, y, xl, core = (lax.axis_index(name) for name in AXES)
    row_id = z * N_XH + xh
    col_id = (y * N_XL + xl) * N_CORE + core
    where = jnp.stack([a_count[0, 0], xh, core, row_id, col_id, z]).astype(jnp.int32)
    tile_vals = a_vals[0, 0]
    place = a_place[0, 0].reshape(-1)
    height, width = res_p.shape[1:]
    p_flat, r_flat = p_cols.reshape(-1), r_cols.reshape(-1)
    tile = shape((height, width))
    slots = tile_vals.shape[0]
    scratch = (
        pltpu.VMEM(tile_vals.shape, jnp.bfloat16),
        pltpu.VMEM((slots, height, width), jnp.bfloat16),
        pltpu.SemaphoreType.DMA((slots,)),
        pltpu.SemaphoreType.DMA((slots,)),
    )

    r_own = gather(res_r, ("y", "xl"), HALF_COL)
    p_own = lax.all_gather(res_p, "z", axis=0, tiled=True)
    p_other = turned(p_own, "xh", 1)
    r_own = after(r_own, p_own)
    r_other = turned(r_own, "core", 1)
    where = after(where, p_own)
    p_plan, r_plan = on_device(
        plan_kernel,
        (shape((4 * slots + 8,), jnp.int32),) * 2,
        (where, place, p_flat, r_flat),
        scalars_out=2,
    )

    *r_thirds, where_then = on_device(
        restrict_kernel,
        (shape((N_ROW // 3, height, width)),) * 3 + (shape(where.shape, jnp.int32),),
        (where, r_plan),
        left=(r_own, r_other, tile_vals),
        scratch=[pltpu.VMEM((N_ROW, height, width), jnp.float32), *scratch],
        cost=COST,
        mib=48,
        scalars_out=1,
    )
    r_thirds = (r_thirds[0], turned(r_thirds[1], "z", -1), turned(r_thirds[2], "z", 1))
    p_mine, p_low, p_high = on_device(
        prolong_kernel,
        (shape((HALF_COL, height, width)),) + (shape((HALF_COL // 2, height, width)),) * 2,
        (where_then, p_plan),
        left=(p_own, p_other, tile_vals),
        scratch=[pltpu.VMEM((N_COL, height, width), jnp.float32), *scratch],
        cost=COST,
        mib=48,
    )
    p_near = (turned(p_low, "core", 1), turned(p_high, "core", 1))

    r_mine, r_theirs = on_device(
        thirds_kernel, (shape((4, height, width)),) * 2, (where,), *r_thirds
    )
    r_near = turned(r_theirs, "xh", 1)
    r_quarters = on_device(halves_kernel, (tile,) * 4, (), r_mine, r_near)
    r_parts = [turned(quarter, "z", -3 * i) for i, quarter in enumerate(r_quarters)]
    p_mine = after(p_mine, r_theirs)
    (p_sum,) = on_device(pair_kernel, (shape((HALF_COL, height, width)),), (), p_mine, *p_near)
    p_parts = [lax.all_to_all(p_sum, ("y", "xl"), 0, 0, tiled=True)]

    component = jnp.tile(null_layout % NS, width // null_layout.shape[0])
    projector = (component[:, None] == component[None, :]).astype(jnp.float32) * (NS / width)
    mass_rows = mass[0][:, None]
    update_p, sums_p = step(p_parts, mass_rows, res_p[0], projector)
    update_r, sums_r = step(r_parts, mass_rows, res_r[0], projector)
    sums = jnp.sum(jnp.concatenate([sums_p, sums_r]), axis=1)
    sums = jnp.pad(sums[None, None], ((0, 0), (0, 0), (0, width - sums.shape[0])))
    sums = gather(sums, ("xh", "xl", "core"), N_XH * N_XL * N_CORE)
    sums = gather(jnp.sum(sums, axis=0, keepdims=True), ("z", "y"), N_Z * N_Y)
    outs = on_device(
        final_kernel,
        (tile,) * 4,
        (),
        sums,
        p_now[0],
        res_p[0],
        update_p,
        rt_now[0],
        res_r[0],
        update_r,
    )
    return tuple(out[None] for out in outs)


def solution(mesh):
    fine = Mesh(mesh.devices.reshape(SIZES), AXES)
    row, col = ("z", "xh"), ("y", "xl", "core")
    tiles = P(row + col, None, None)
    in_specs = (
        P(row, col, None, None, None),
        P(row, col, None, None),
        P(row, col),
        P(),
        P(),
        P(),
        P(row + col, None),
        tiles,
        tiles,
        tiles,
        tiles,
    )
    return jax.shard_map(
        shards, mesh=fine, in_specs=in_specs, out_specs=(tiles,) * 4, check_vma=False
    )
```

```python
import functools

import jax
import jax.numpy as jnp
from jax import lax
from jax.experimental import pallas as pl
from jax.experimental.pallas import tpu as pltpu
from jax.sharding import Mesh
from jax.sharding import PartitionSpec as P

NS = 4
EPSILON = 1e-06
EXACT = lax.Precision.HIGHEST

SIZES = (12, 2, 8, 2, 2)
AXES = ("z", "xh", "y", "xl", "core")
N_Z, N_XH, N_Y, N_XL, N_CORE = SIZES
N_ROW, N_COL = N_Z * N_XH, N_Y * N_XL * N_CORE
HALF_COL = N_COL // 2
SWAP = ((0, 1), (1, 0))

VMEM = pl.BlockSpec(memory_space=pltpu.VMEM)
HBM = pl.BlockSpec(memory_space=pltpu.HBM)
SMEM = pl.BlockSpec(memory_space=pltpu.SMEM)
COST = pl.CostEstimate(flops=2**29, bytes_accessed=12 * 2**20, transcendentals=0)
MIB = 2**20


def matches(cols_ref, source, target):
    s0, s1 = cols_ref[0, source], cols_ref[1, source]
    t0, t1 = cols_ref[0, target], cols_ref[1, target]
    flag = lambda same, bit: jnp.where(same, bit, 0)
    return flag(s0 == t0, 1) + flag(s1 == t1, 2) + flag(s1 == t0, 4) + flag(s0 == t1, 8)


def plan_kernel(where_ref, place_ref, p_cols_ref, r_cols_ref, p_plan_ref, r_plan_ref):
    count, xh, core = where_ref[0], where_ref[1], where_ref[2]
    row_id, col_id = where_ref[3], where_ref[4]
    slots = place_ref.shape[1]

    def note(plan_ref, used, slot, target, index, blocks):
        for field, value in enumerate((slot, target, index, blocks)):
            plan_ref[field * slots + used] = value
        return used + jnp.where(blocks != 0, 1, 0)

    def body(a, used):
        local_row, local_col = place_ref[0, a], place_ref[1, a]
        tile_row = row_id * N_COL + local_row
        tile_col = local_col * N_COL + col_id
        p_index = local_col // N_XH + jnp.where(lax.rem(local_col, N_XH) == xh, 0, N_Z)
        r_index = local_row // N_CORE + jnp.where(lax.rem(local_row, N_CORE) == core, 0, HALF_COL)
        p_blocks = matches(p_cols_ref, tile_col, tile_row)
        r_blocks = matches(r_cols_ref, tile_row, tile_col)
        return (
            note(p_plan_ref, used[0], a, local_row, p_index, p_blocks),
            note(r_plan_ref, used[1], a, local_col, r_index, r_blocks),
        )

    p_used, r_used = lax.fori_loop(0, count, body, (0, 0))
    p_plan_ref[4 * slots] = p_used
    r_plan_ref[4 * slots] = r_used


def clear(acc_ref):
    def body(i, carry):
        acc_ref[i] = jnp.zeros(acc_ref.shape[1:], acc_ref.dtype)
        return carry

    lax.fori_loop(0, acc_ref.shape[0], body, 0)


def add_columns(acc_ref, index, whole, blocks):
    block = whole.shape[1] // 2
    left = lax.broadcasted_iota(jnp.int32, (1, whole.shape[1]), 1) < block

    @pl.when((blocks & 3) != 0)
    def _():
        keep = jnp.where(left, blocks & 1, blocks & 2) != 0
        acc_ref[index] += jnp.where(keep, whole, 0.0)

    @pl.when((blocks & 12) != 0)
    def _():
        keep = jnp.where(left, blocks & 4, blocks & 8) != 0
        acc_ref[index] += jnp.where(keep, pltpu.roll(whole, block, 1), 0.0)


def each_used(plan_ref, own_ref, other_ref, a_ref, scratch, product, whole):
    acc_ref, held_ref, tiles_ref, held_sems, tile_sems = scratch
    slots, own_count = a_ref.shape[0], own_ref.shape[0]
    used = plan_ref[4 * slots]
    hold = lambda k: pltpu.make_async_copy(
        a_ref.at[plan_ref[k]], held_ref.at[k], held_sems.at[k]
    )
    take = lambda k, ref, index: pltpu.make_async_copy(
        ref.at[index], tiles_ref.at[k], tile_sems.at[k]
    )
    large = []
    if whole:
        large.append(pltpu.make_async_copy(a_ref, held_ref, held_sems.at[0]))
        for i, ref in enumerate((own_ref, other_ref)):
            part = tiles_ref.at[pl.ds(i * own_count, own_count)]
            large.append(pltpu.make_async_copy(ref, part, tile_sems.at[i]))

    def start(k, carry):
        index = plan_ref[2 * slots + k]

        @pl.when(index < own_count)
        def _():
            take(k, own_ref, index).start()

        @pl.when(index >= own_count)
        def _():
            take(k, other_ref, index - own_count).start()

        hold(k).start()
        return carry

    def finish(k, carry):
        if whole:
            held, tile = plan_ref[k], plan_ref[2 * slots + k]
        else:
            held, tile = k, k
            take(k, own_ref, 0).wait()
            hold(k).wait()
        result = product(held_ref[held], tiles_ref[tile])
        add_columns(acc_ref, plan_ref[slots + k], result, plan_ref[3 * slots + k])
        return carry

    if whole:
        for copy in large:
            copy.start()
    else:
        lax.fori_loop(0, used, start, 0)
    clear(acc_ref)
    if whole:
        for copy in large:
            copy.wait()
    lax.fori_loop(0, used, finish, 0)


def prolong_kernel(
    where_ref,
    plan_ref,
    own_ref,
    other_ref,
    a_ref,
    mine_ref,
    theirs_low_ref,
    theirs_high_ref,
    *scratch,
):
    core = where_ref[2]
    acc_ref = scratch[0]
    product = functools.partial(jnp.dot, preferred_element_type=jnp.float32)
    each_used(plan_ref, own_ref, other_ref, a_ref, scratch, product, True)

    def store(q, carry):
        mine_ref[q] = acc_ref[2 * q + core].astype(jnp.bfloat16)
        return carry

    lax.fori_loop(0, HALF_COL, store, 0)

    def store_theirs(q, carry):
        theirs_low_ref[q] = acc_ref[2 * q + 1 - core].astype(jnp.bfloat16)
        theirs_high_ref[q] = acc_ref[HALF_COL + 2 * q + 1 - core].astype(jnp.bfloat16)
        return carry

    lax.fori_loop(0, HALF_COL // 2, store_theirs, 0)


def restrict_kernel(
    where_ref,
    plan_ref,
    own_ref,
    other_ref,
    a_ref,
    own_third_ref,
    up_third_ref,
    down_third_ref,
    after_ref,
    *scratch,
):
    for i in range(where_ref.shape[0]):
        after_ref[i] = where_ref[i]
    z, acc_ref = where_ref[5], scratch[0]

    def product(block, tile):
        return lax.dot_general(
            block, tile, (((0,), (0,)), ((), ())), preferred_element_type=jnp.float32
        )

    each_used(plan_ref, own_ref, other_ref, a_ref, scratch, product, False)

    def store(q, carry):
        for third, ref in enumerate((own_third_ref, up_third_ref, down_third_ref)):
            owner = 3 * (q // N_XH) + lax.rem(z + third, 3)
            ref[q] = acc_ref[N_XH * owner + lax.rem(q, N_XH)].astype(jnp.bfloat16)
        return carry

    lax.fori_loop(0, N_ROW // 3, store, 0)


def wide_sum(refs, index):
    total = refs[0][index].astype(jnp.float32)
    for ref in refs[1:]:
        total += ref[index].astype(jnp.float32)
    return total.astype(jnp.bfloat16)


def pair_kernel(mine_ref, near_low_ref, near_high_ref, sum_ref):
    half = near_low_ref.shape[0]

    def body(i, carry):
        for start, near_ref in ((0, near_low_ref), (half, near_high_ref)):
            total = mine_ref[start + i].astype(jnp.float32) + near_ref[i].astype(jnp.float32)
            sum_ref[start + i] = total.astype(jnp.bfloat16)
        return carry

    lax.fori_loop(0, half, body, 0)


def thirds_kernel(where_ref, own_ref, up_ref, down_ref, mine_ref, theirs_ref):
    quarter, xh = where_ref[5] // 3, where_ref[1]
    for i in range(mine_ref.shape[0]):
        index = N_XH * lax.rem(quarter + i, 4)
        mine_ref[i] = wide_sum((own_ref, up_ref, down_ref), index + xh)
        theirs_ref[i] = wide_sum((own_ref, up_ref, down_ref), index + 1 - xh)


def halves_kernel(mine_ref, near_ref, *quarter_refs):
    for i, ref in enumerate(quarter_refs):
        ref[...] = wide_sum((mine_ref, near_ref), i)


def update_kernel(mass_ref, resid_ref, projector_ref, *refs):
    update_ref, sums_ref = refs[-2:]
    resid = resid_ref[...].astype(jnp.float32)
    full = mass_ref[...] * resid
    for parts_ref in refs[:-2]:
        if len(parts_ref.shape) == 2:
            full += parts_ref[...].astype(jnp.float32)
        else:
            add = lambda i, total, ref=parts_ref: total + ref[i].astype(jnp.float32)
            full = lax.fori_loop(0, parts_ref.shape[0], add, full)
    update = full - jnp.dot(
        full, projector_ref[...], precision=EXACT, preferred_element_type=jnp.float32
    )
    update_ref[...] = update
    sums_ref[0:1, :] = jnp.sum(update * resid, axis=0, keepdims=True)
    sums_ref[1:2, :] = jnp.sum(update * update, axis=0, keepdims=True)


def shape(dims, dtype=jnp.bfloat16):
    return jax.ShapeDtypeStruct(dims, dtype)


def on_device(
    kernel, out_shape, scalars, *operands, left=(), scratch=(), cost=None, scalars_out=0, mib=6
):
    count = len(out_shape)
    return pl.pallas_call(
        kernel,
        out_shape=out_shape,
        in_specs=[SMEM] * len(scalars) + [VMEM] * len(operands) + [HBM] * len(left),
        out_specs=(VMEM,) * (count - scalars_out) + (SMEM,) * scalars_out,
        scratch_shapes=scratch,
        cost_estimate=cost,
        compiler_params=pltpu.CompilerParams(vmem_limit_bytes=mib * MIB),
    )(*scalars, *operands, *left)


def after(array, *earlier):
    return pl.pallas_call(
        lambda *refs: None,
        out_shape=shape(array.shape, array.dtype),
        in_specs=[pl.BlockSpec(memory_space=pl.ANY)] * (1 + len(earlier)),
        out_specs=pl.BlockSpec(memory_space=pl.ANY),
        input_output_aliases={0: 0},
        compiler_params=pltpu.CompilerParams(vmem_limit_bytes=MIB),
    )(array, *earlier)


def step(parts, mass_rows, resid, projector):
    return on_device(
        update_kernel,
        (shape(resid.shape, jnp.float32), shape((2, resid.shape[1]), jnp.float32)),
        (),
        mass_rows,
        resid,
        projector,
        *parts,
    )


def turned(array, axis, by):
    size = lax.axis_size(axis)
    if by % size == 0:
        return array
    return lax.ppermute(array, axis, [((i + by) % size, i) for i in range(size)])


def gather(tile, axes, count):
    copies = jnp.broadcast_to(tile, (count,) + tile.shape[1:])
    return lax.all_to_all(copies, axes, 0, 0, tiled=True)


def final_kernel(
    sums_ref,
    p_now_ref,
    res_p_ref,
    update_p_ref,
    rt_now_ref,
    res_r_ref,
    update_r_ref,
    p_next_ref,
    res_p_next_ref,
    rt_next_ref,
    res_r_next_ref,
):
    sums = jnp.sum(sums_ref[...], axis=0)
    alpha_p = sums[0:1, 0:1] / (sums[0:1, 1:2] + EPSILON)
    alpha_r = sums[0:1, 2:3] / (sums[0:1, 3:4] + EPSILON)
    for alpha, now_ref, res_ref, update_ref, next_ref, res_next_ref in (
        (alpha_p, p_now_ref, res_p_ref, update_p_ref, p_next_ref, res_p_next_ref),
        (alpha_r, rt_now_ref, res_r_ref, update_r_ref, rt_next_ref, res_r_next_ref),
    ):
        resid = res_ref[...].astype(jnp.float32)
        next_ref[...] = (now_ref[...].astype(jnp.float32) + alpha * resid).astype(jnp.bfloat16)
        res_next_ref[...] = (resid - alpha * update_ref[...]).astype(jnp.bfloat16)


def shards(
    a_vals, a_place, a_count, p_cols, r_cols, null_layout, mass, p_now, res_p, rt_now, res_r
):
    z, xh, y, xl, core = (lax.axis_index(name) for name in AXES)
    row_id = z * N_XH + xh
    col_id = (y * N_XL + xl) * N_CORE + core
    where = jnp.stack([a_count[0, 0], xh, core, row_id, col_id, z]).astype(jnp.int32)
    tile_vals = a_vals[0, 0]
    place = a_place[0, 0]
    height, width = res_p.shape[1:]
    tile = shape((height, width))
    slots = tile_vals.shape[0]
    scratch = (
        pltpu.VMEM(tile_vals.shape, jnp.bfloat16),
        pltpu.VMEM((max(slots, N_COL, N_ROW), height, width), jnp.bfloat16),
        pltpu.SemaphoreType.DMA((slots,)),
        pltpu.SemaphoreType.DMA((slots,)),
    )

    r_own = gather(res_r, ("y", "xl"), HALF_COL)
    p_own = lax.all_gather(res_p, "z", axis=0, tiled=True)
    p_other = turned(p_own, "xh", 1)
    r_own = after(r_own, p_own)
    r_other = turned(r_own, "core", 1)
    where = after(where, p_own)
    p_plan, r_plan = on_device(
        plan_kernel,
        (shape((4 * slots + 8,), jnp.int32),) * 2,
        (where, place, p_cols.T, r_cols.T),
        scalars_out=2,
    )

    *r_thirds, where_then = on_device(
        restrict_kernel,
        (shape((N_ROW // 3, height, width)),) * 3 + (shape(where.shape, jnp.int32),),
        (where, r_plan),
        left=(r_own, r_other, tile_vals),
        scratch=[pltpu.VMEM((N_ROW, height, width), jnp.float32), *scratch],
        cost=COST,
        mib=48,
        scalars_out=1,
    )
    r_thirds = (r_thirds[0], turned(r_thirds[1], "z", -1), turned(r_thirds[2], "z", 1))
    p_mine, p_low, p_high = on_device(
        prolong_kernel,
        (shape((HALF_COL, height, width)),) + (shape((HALF_COL // 2, height, width)),) * 2,
        (where_then, p_plan),
        left=(p_own, p_other, tile_vals),
        scratch=[pltpu.VMEM((N_COL, height, width), jnp.float32), *scratch],
        cost=COST,
        mib=48,
    )
    p_near = (turned(p_low, "core", 1), turned(p_high, "core", 1))

    r_mine, r_theirs = on_device(
        thirds_kernel, (shape((4, height, width)),) * 2, (where,), *r_thirds
    )
    r_near = turned(r_theirs, "xh", 1)
    r_quarters = on_device(halves_kernel, (tile,) * 4, (), r_mine, r_near)
    r_parts = [turned(quarter, "z", -3 * i) for i, quarter in enumerate(r_quarters)]
    p_mine = after(p_mine, r_theirs)
    (p_sum,) = on_device(pair_kernel, (shape((HALF_COL, height, width)),), (), p_mine, *p_near)
    p_parts = [lax.all_to_all(p_sum, ("y", "xl"), 0, 0, tiled=True)]

    component = jnp.tile(null_layout % NS, width // null_layout.shape[0])
    projector = (component[:, None] == component[None, :]).astype(jnp.float32) * (NS / width)
    mass_rows = mass[0][:, None]
    update_p, sums_p = step(p_parts, mass_rows, res_p[0], projector)
    update_r, sums_r = step(r_parts, mass_rows, res_r[0], projector)
    sums = jnp.sum(jnp.concatenate([sums_p, sums_r]), axis=1)
    sums = jnp.pad(sums[None, None], ((0, 0), (0, 0), (0, width - sums.shape[0])))
    sums = gather(sums, ("xh", "xl", "core"), N_XH * N_XL * N_CORE)
    sums = gather(jnp.sum(sums, axis=0, keepdims=True), ("z", "y"), N_Z * N_Y)
    outs = on_device(
        final_kernel,
        (tile,) * 4,
        (),
        sums,
        p_now[0],
        res_p[0],
        update_p,
        rt_now[0],
        res_r[0],
        update_r,
    )
    return tuple(out[None] for out in outs)


def solution(mesh):
    fine = Mesh(mesh.devices.reshape(SIZES), AXES)
    row, col = ("z", "xh"), ("y", "xl", "core")
    tiles = P(row + col, None, None)
    in_specs = (
        P(row, col, None, None, None),
        P(row, col, None, None),
        P(row, col),
        P(),
        P(),
        P(),
        P(row + col, None),
        tiles,
        tiles,
        tiles,
        tiles,
    )
    return jax.shard_map(
        shards, mesh=fine, in_specs=in_specs, out_specs=(tiles,) * 4, check_vma=False
    )
```

```python
import functools

import jax
import jax.numpy as jnp
from jax import lax
from jax.experimental import pallas as pl
from jax.experimental.pallas import tpu as pltpu
from jax.sharding import Mesh
from jax.sharding import PartitionSpec as P

NS = 4
EPSILON = 1e-06
EXACT = lax.Precision.HIGHEST

SIZES = (12, 2, 8, 2, 2)
AXES = ("z", "xh", "y", "xl", "core")
N_Z, N_XH, N_Y, N_XL, N_CORE = SIZES
N_ROW, N_COL = N_Z * N_XH, N_Y * N_XL * N_CORE
HALF_COL = N_COL // 2
SWAP = ((0, 1), (1, 0))

VMEM = pl.BlockSpec(memory_space=pltpu.VMEM)
HBM = pl.BlockSpec(memory_space=pltpu.HBM)
SMEM = pl.BlockSpec(memory_space=pltpu.SMEM)
COST = pl.CostEstimate(flops=2**29, bytes_accessed=12 * 2**20, transcendentals=0)
MIB = 2**20


def matches(cols_ref, source, target):
    s0, s1 = cols_ref[0, source], cols_ref[1, source]
    t0, t1 = cols_ref[0, target], cols_ref[1, target]
    flag = lambda same, bit: jnp.where(same, bit, 0)
    return flag(s0 == t0, 1) + flag(s1 == t1, 2) + flag(s1 == t0, 4) + flag(s0 == t1, 8)


def plan_kernel(where_ref, place_ref, p_cols_ref, r_cols_ref, p_plan_ref, r_plan_ref):
    count, xh, core = where_ref[0], where_ref[1], where_ref[2]
    row_id, col_id = where_ref[3], where_ref[4]
    slots = place_ref.shape[1]

    def note(plan_ref, used, slot, target, index, blocks):
        for field, value in enumerate((slot, target, index, blocks)):
            plan_ref[field * slots + used] = value
        return used + jnp.where(blocks != 0, 1, 0)

    def body(a, used):
        local_row, local_col = place_ref[0, a], place_ref[1, a]
        tile_row = row_id * N_COL + local_row
        tile_col = local_col * N_COL + col_id
        p_index = local_col // N_XH + jnp.where(lax.rem(local_col, N_XH) == xh, 0, N_Z)
        r_index = local_row // N_CORE + jnp.where(lax.rem(local_row, N_CORE) == core, 0, HALF_COL)
        p_blocks = matches(p_cols_ref, tile_col, tile_row)
        r_blocks = matches(r_cols_ref, tile_row, tile_col)
        return (
            note(p_plan_ref, used[0], a, local_row, p_index, p_blocks),
            note(r_plan_ref, used[1], a, local_col, r_index, r_blocks),
        )

    p_used, r_used = lax.fori_loop(0, count, body, (0, 0))
    p_plan_ref[4 * slots] = p_used
    r_plan_ref[4 * slots] = r_used


def clear(acc_ref):
    def body(i, carry):
        acc_ref[i] = jnp.zeros(acc_ref.shape[1:], acc_ref.dtype)
        return carry

    lax.fori_loop(0, acc_ref.shape[0], body, 0)


def add_columns(acc_ref, index, whole, blocks):
    block = whole.shape[1] // 2
    left = lax.broadcasted_iota(jnp.int32, (1, whole.shape[1]), 1) < block

    @pl.when((blocks & 3) != 0)
    def _():
        keep = jnp.where(left, blocks & 1, blocks & 2) != 0
        acc_ref[index] += jnp.where(keep, whole, 0.0)

    @pl.when((blocks & 12) != 0)
    def _():
        keep = jnp.where(left, blocks & 4, blocks & 8) != 0
        acc_ref[index] += jnp.where(keep, pltpu.roll(whole, block, 1), 0.0)


def each_used(plan_ref, own_ref, other_ref, a_ref, scratch, product):
    acc_ref, held_ref, tiles_ref, held_sems, tile_sems = scratch
    slots, own_count = a_ref.shape[0], own_ref.shape[0]
    used = plan_ref[4 * slots]
    hold = lambda k: pltpu.make_async_copy(
        a_ref.at[plan_ref[k]], held_ref.at[k], held_sems.at[k]
    )
    take = lambda k, ref, index: pltpu.make_async_copy(
        ref.at[index], tiles_ref.at[k], tile_sems.at[k]
    )

    def start(k, carry):
        index = plan_ref[2 * slots + k]

        @pl.when(index < own_count)
        def _():
            take(k, own_ref, index).start()

        @pl.when(index >= own_count)
        def _():
            take(k, other_ref, index - own_count).start()

        hold(k).start()
        return carry

    def finish(k, carry):
        take(k, own_ref, 0).wait()
        hold(k).wait()
        whole = product(held_ref[k], tiles_ref[k])
        add_columns(acc_ref, plan_ref[slots + k], whole, plan_ref[3 * slots + k])
        return carry

    lax.fori_loop(0, used, start, 0)
    clear(acc_ref)
    lax.fori_loop(0, used, finish, 0)


def prolong_kernel(
    where_ref,
    plan_ref,
    own_ref,
    other_ref,
    a_ref,
    mine_ref,
    theirs_low_ref,
    theirs_high_ref,
    *scratch,
):
    core = where_ref[2]
    acc_ref = scratch[0]
    product = functools.partial(jnp.dot, preferred_element_type=jnp.float32)
    each_used(plan_ref, own_ref, other_ref, a_ref, scratch, product)

    def store(q, carry):
        mine_ref[q] = acc_ref[2 * q + core].astype(jnp.bfloat16)
        return carry

    lax.fori_loop(0, HALF_COL, store, 0)

    def store_theirs(q, carry):
        theirs_low_ref[q] = acc_ref[2 * q + 1 - core].astype(jnp.bfloat16)
        theirs_high_ref[q] = acc_ref[HALF_COL + 2 * q + 1 - core].astype(jnp.bfloat16)
        return carry

    lax.fori_loop(0, HALF_COL // 2, store_theirs, 0)


def restrict_kernel(
    where_ref,
    plan_ref,
    own_ref,
    other_ref,
    a_ref,
    own_third_ref,
    up_third_ref,
    down_third_ref,
    after_ref,
    *scratch,
):
    for i in range(where_ref.shape[0]):
        after_ref[i] = where_ref[i]
    z, acc_ref = where_ref[5], scratch[0]

    def product(block, tile):
        return lax.dot_general(
            block, tile, (((0,), (0,)), ((), ())), preferred_element_type=jnp.float32
        )

    each_used(plan_ref, own_ref, other_ref, a_ref, scratch, product)

    def store(q, carry):
        for third, ref in enumerate((own_third_ref, up_third_ref, down_third_ref)):
            owner = 3 * (q // N_XH) + lax.rem(z + third, 3)
            ref[q] = acc_ref[N_XH * owner + lax.rem(q, N_XH)].astype(jnp.bfloat16)
        return carry

    lax.fori_loop(0, N_ROW // 3, store, 0)


def wide_sum(refs, index):
    total = refs[0][index].astype(jnp.float32)
    for ref in refs[1:]:
        total += ref[index].astype(jnp.float32)
    return total.astype(jnp.bfloat16)


def pair_kernel(mine_ref, near_low_ref, near_high_ref, sum_ref):
    half = near_low_ref.shape[0]

    def body(i, carry):
        for start, near_ref in ((0, near_low_ref), (half, near_high_ref)):
            total = mine_ref[start + i].astype(jnp.float32) + near_ref[i].astype(jnp.float32)
            sum_ref[start + i] = total.astype(jnp.bfloat16)
        return carry

    lax.fori_loop(0, half, body, 0)


def thirds_kernel(where_ref, own_ref, up_ref, down_ref, mine_ref, theirs_ref):
    quarter, xh = where_ref[5] // 3, where_ref[1]
    for i in range(mine_ref.shape[0]):
        index = N_XH * lax.rem(quarter + i, 4)
        mine_ref[i] = wide_sum((own_ref, up_ref, down_ref), index + xh)
        theirs_ref[i] = wide_sum((own_ref, up_ref, down_ref), index + 1 - xh)


def halves_kernel(mine_ref, near_ref, *quarter_refs):
    for i, ref in enumerate(quarter_refs):
        ref[...] = wide_sum((mine_ref, near_ref), i)


def update_kernel(mass_ref, resid_ref, projector_ref, *refs):
    update_ref, sums_ref = refs[-2:]
    resid = resid_ref[...].astype(jnp.float32)
    full = mass_ref[...] * resid
    for parts_ref in refs[:-2]:
        if len(parts_ref.shape) == 2:
            full += parts_ref[...].astype(jnp.float32)
        else:
            add = lambda i, total, ref=parts_ref: total + ref[i].astype(jnp.float32)
            full = lax.fori_loop(0, parts_ref.shape[0], add, full)
    update = full - jnp.dot(
        full, projector_ref[...], precision=EXACT, preferred_element_type=jnp.float32
    )
    update_ref[...] = update
    sums_ref[0:1, :] = jnp.sum(update * resid, axis=0, keepdims=True)
    sums_ref[1:2, :] = jnp.sum(update * update, axis=0, keepdims=True)


def shape(dims, dtype=jnp.bfloat16):
    return jax.ShapeDtypeStruct(dims, dtype)


def on_device(
    kernel, out_shape, scalars, *operands, left=(), scratch=(), cost=None, scalars_out=0, mib=6
):
    count = len(out_shape)
    return pl.pallas_call(
        kernel,
        out_shape=out_shape,
        in_specs=[SMEM] * len(scalars) + [VMEM] * len(operands) + [HBM] * len(left),
        out_specs=(VMEM,) * (count - scalars_out) + (SMEM,) * scalars_out,
        scratch_shapes=scratch,
        cost_estimate=cost,
        compiler_params=pltpu.CompilerParams(vmem_limit_bytes=mib * MIB),
    )(*scalars, *operands, *left)


def after(array, *earlier):
    return pl.pallas_call(
        lambda *refs: None,
        out_shape=shape(array.shape, array.dtype),
        in_specs=[pl.BlockSpec(memory_space=pl.ANY)] * (1 + len(earlier)),
        out_specs=pl.BlockSpec(memory_space=pl.ANY),
        input_output_aliases={0: 0},
        compiler_params=pltpu.CompilerParams(vmem_limit_bytes=MIB),
    )(array, *earlier)


def step(parts, mass_rows, resid, projector):
    return on_device(
        update_kernel,
        (shape(resid.shape, jnp.float32), shape((2, resid.shape[1]), jnp.float32)),
        (),
        mass_rows,
        resid,
        projector,
        *parts,
    )


def turned(array, axis, by):
    size = lax.axis_size(axis)
    if by % size == 0:
        return array
    return lax.ppermute(array, axis, [((i + by) % size, i) for i in range(size)])


def gather(tile, axes, count):
    copies = jnp.broadcast_to(tile, (count,) + tile.shape[1:])
    return lax.all_to_all(copies, axes, 0, 0, tiled=True)


def final_kernel(
    sums_ref,
    p_now_ref,
    res_p_ref,
    update_p_ref,
    rt_now_ref,
    res_r_ref,
    update_r_ref,
    p_next_ref,
    res_p_next_ref,
    rt_next_ref,
    res_r_next_ref,
):
    sums = jnp.sum(sums_ref[...], axis=0)
    alpha_p = sums[0:1, 0:1] / (sums[0:1, 1:2] + EPSILON)
    alpha_r = sums[0:1, 2:3] / (sums[0:1, 3:4] + EPSILON)
    for alpha, now_ref, res_ref, update_ref, next_ref, res_next_ref in (
        (alpha_p, p_now_ref, res_p_ref, update_p_ref, p_next_ref, res_p_next_ref),
        (alpha_r, rt_now_ref, res_r_ref, update_r_ref, rt_next_ref, res_r_next_ref),
    ):
        resid = res_ref[...].astype(jnp.float32)
        next_ref[...] = (now_ref[...].astype(jnp.float32) + alpha * resid).astype(jnp.bfloat16)
        res_next_ref[...] = (resid - alpha * update_ref[...]).astype(jnp.bfloat16)


def shards(
    a_vals, a_place, a_count, p_cols, r_cols, null_layout, mass, p_now, res_p, rt_now, res_r
):
    z, xh, y, xl, core = (lax.axis_index(name) for name in AXES)
    row_id = z * N_XH + xh
    col_id = (y * N_XL + xl) * N_CORE + core
    where = jnp.stack([a_count[0, 0], xh, core, row_id, col_id, z]).astype(jnp.int32)
    tile_vals = a_vals[0, 0]
    place = a_place[0, 0]
    height, width = res_p.shape[1:]
    tile = shape((height, width))
    slots = tile_vals.shape[0]
    scratch = (
        pltpu.VMEM(tile_vals.shape, jnp.bfloat16),
        pltpu.VMEM((slots, height, width), jnp.bfloat16),
        pltpu.SemaphoreType.DMA((slots,)),
        pltpu.SemaphoreType.DMA((slots,)),
    )

    r_own = gather(res_r, ("y", "xl"), HALF_COL)
    p_own = lax.all_gather(res_p, "z", axis=0, tiled=True)
    p_other = turned(p_own, "xh", 1)
    r_own = after(r_own, p_own)
    r_other = turned(r_own, "core", 1)
    where = after(where, p_own)
    p_plan, r_plan = on_device(
        plan_kernel,
        (shape((4 * slots + 8,), jnp.int32),) * 2,
        (where, place, p_cols.T, r_cols.T),
        scalars_out=2,
    )

    *r_thirds, where_then = on_device(
        restrict_kernel,
        (shape((N_ROW // 3, height, width)),) * 3 + (shape(where.shape, jnp.int32),),
        (where, r_plan),
        left=(r_own, r_other, tile_vals),
        scratch=[pltpu.VMEM((N_ROW, height, width), jnp.float32), *scratch],
        cost=COST,
        mib=48,
        scalars_out=1,
    )
    r_thirds = (r_thirds[0], turned(r_thirds[1], "z", -1), turned(r_thirds[2], "z", 1))
    p_mine, p_low, p_high = on_device(
        prolong_kernel,
        (shape((HALF_COL, height, width)),) + (shape((HALF_COL // 2, height, width)),) * 2,
        (where_then, p_plan),
        left=(p_own, p_other, tile_vals),
        scratch=[pltpu.VMEM((N_COL, height, width), jnp.float32), *scratch],
        cost=COST,
        mib=48,
    )
    p_near = (turned(p_low, "core", 1), turned(p_high, "core", 1))

    r_mine, r_theirs = on_device(
        thirds_kernel, (shape((4, height, width)),) * 2, (where,), *r_thirds
    )
    r_near = turned(r_theirs, "xh", 1)
    r_quarters = on_device(halves_kernel, (tile,) * 4, (), r_mine, r_near)
    r_parts = [turned(r_quarters[i], "z", -3 * i) for i in (2, 1, 3, 0)]
    p_mine = after(p_mine, r_theirs)
    (p_sum,) = on_device(pair_kernel, (shape((HALF_COL, height, width)),), (), p_mine, *p_near)
    p_parts = [lax.all_to_all(p_sum, ("y", "xl"), 0, 0, tiled=True)]

    component = jnp.tile(null_layout % NS, width // null_layout.shape[0])
    projector = (component[:, None] == component[None, :]).astype(jnp.float32) * (NS / width)
    mass_rows = mass[0][:, None]
    update_p, sums_p = step(p_parts, mass_rows, res_p[0], projector)
    update_r, sums_r = step(r_parts, mass_rows, res_r[0], projector)
    sums = jnp.sum(jnp.concatenate([sums_p, sums_r]), axis=1)
    sums = jnp.pad(sums[None, None], ((0, 0), (0, 0), (0, width - sums.shape[0])))
    sums = gather(sums, ("xh", "xl", "core"), N_XH * N_XL * N_CORE)
    sums = gather(jnp.sum(sums, axis=0, keepdims=True), ("z", "y"), N_Z * N_Y)
    outs = on_device(
        final_kernel,
        (tile,) * 4,
        (),
        sums,
        p_now[0],
        res_p[0],
        update_p,
        rt_now[0],
        res_r[0],
        update_r,
    )
    return tuple(out[None] for out in outs)


def solution(mesh):
    fine = Mesh(mesh.devices.reshape(SIZES), AXES)
    row, col = ("z", "xh"), ("y", "xl", "core")
    tiles = P(row + col, None, None)
    in_specs = (
        P(row, col, None, None, None),
        P(row, col, None, None),
        P(row, col),
        P(),
        P(),
        P(),
        P(row + col, None),
        tiles,
        tiles,
        tiles,
        tiles,
    )
    return jax.shard_map(
        shards, mesh=fine, in_specs=in_specs, out_specs=(tiles,) * 4, check_vma=False
    )
```
